128 devices in a mesh: region: 16 (over z, y), dom: 8 (over x, core).
Axes of the slice: x: 4, y: 4, z: 4, core: 2. Of those that a mesh axis runs over, the one named last changes fastest.
Arguments:
- x_start: float32 [131072, 128], P(('region', 'dom')), may hold values from -300 to 300
- p_start: float32 [131072, 128], P(('region', 'dom')), may hold values from -150 to 150
- tiles: bfloat16 [128, 40, 128, 128], P(('region', 'dom')), may hold values from -3 to 3
- tile_row: int32 [128, 40], P(('region', 'dom')), may hold values from 0 to 7, as said below
- tile_col: int32 [128, 40], P(('region', 'dom')), may hold values from 0 to 23, as said below
- tile_count: int32 [128], P(('region', 'dom')), may hold values from 24 to 40, as said below
- send_rows: int32 [128, 4, 512], P(('region', 'dom')), may hold values from 0 to 1023
Outputs:
- vectors: float32 [131072, 128], P(('region', 'dom'))
- direction: float32 [131072, 128], P(('region', 'dom'))
The draws below stay inside these ranges and needn't reach their ends.
Inputs may be any that keep to these rules, and one draw needn't show every extreme that they name: `tile_row`: slot b < 8 of every domain holds row block b and column block b. `tile_col`: slot b < 8 of every domain multiplies block b, and slot 8 + j for j < 16 multiplies block 8 + j. `tile_count`: some domain has 40 live slots and some has 24.
All inputs are finite; a program needn't handle non-finite values.
Results may differ from the reference program's by a relative error of at most 0.0022.
The reference program's roundings to bfloat16 on the way count: a program that leaves them out, or rounds other values in their place, can miss the bound.
Values may be sent and summed in bfloat16 or wider, within the bound.
No kernel may reach another device: no remote copies, remote signals or barrier semaphores. Data moves between devices by JAX's collectives and lax.ppermute only.
A program may use at most 128 MiB of HBM per device.

```python
import math
import jax
import jax.numpy as jnp
from jax import lax

K = 128
TB = 128
NB = 8
HB = 4
ITERS = 3
QSTEPS = 3
NODES_DEV = 1024
HALO = 512
CAP = 40
EXT_B = 24
DOMAINS = 128
NODES = 131072
N_REGION = 16
N_DOM = 8


def domain_weight(key):
    pick_key = jax.random.fold_in(key, 5)
    heavy = jax.random.randint(pick_key, (), 0, DOMAINS, dtype=jnp.int32)
    owners = jnp.arange(NODES, dtype=jnp.int32) // NODES_DEV
    return jnp.where(owners == heavy, 6.0, 1.0).astype(jnp.float32)[:, None]


def draw_x_start(key, part):
    weight = domain_weight(key)
    key = jax.random.fold_in(key, 11)
    first, second = jax.random.split(key, 2)
    spread = jnp.exp(jax.random.uniform(first, (NODES, 1), dtype=jnp.float32) * math.log(10.0))
    entries = jnp.clip(jax.random.normal(second, (NODES, K), dtype=jnp.float32), -5.0, 5.0)
    return (weight * spread * entries).astype(jnp.float32)


def draw_p_start(key, part):
    weight = domain_weight(key)
    key = jax.random.fold_in(key, 13)
    first, second = jax.random.split(key, 2)
    spread = jnp.exp(jax.random.uniform(first, (NODES, 1), dtype=jnp.float32) * math.log(10.0))
    entries = jnp.clip(jax.random.normal(second, (NODES, K), dtype=jnp.float32), -5.0, 5.0)
    return (0.5 * weight * spread * entries).astype(jnp.float32)


def draw_tiles(key, part):
    key = jax.random.fold_in(key, 17)
    noise = jnp.clip(jax.random.normal(key, (DOMAINS, CAP, TB, TB), dtype=jnp.float32), -4.0, 4.0)
    noise = noise / math.sqrt(TB)
    slot_ids = jnp.arange(CAP)[None, :, None, None]
    identity = jnp.eye(TB, dtype=jnp.float32)[None, None, :, :]
    diagonal = jnp.where(slot_ids < NB, 1.5, 0.0) * identity
    return (noise + diagonal).astype(jnp.bfloat16)


def draw_tile_row(key, part):
    key = jax.random.fold_in(key, 21)
    picks = jax.random.randint(key, (DOMAINS, CAP), 0, NB, dtype=jnp.int32)
    slot_ids = jnp.arange(CAP, dtype=jnp.int32)[None, :]
    return jnp.where(slot_ids < NB, slot_ids, picks).astype(jnp.int32)


def draw_tile_col(key, part):
    key = jax.random.fold_in(key, 23)
    picks = jax.random.randint(key, (DOMAINS, CAP), 0, EXT_B, dtype=jnp.int32)
    slot_ids = jnp.arange(CAP, dtype=jnp.int32)[None, :]
    fixed = jnp.broadcast_to(slot_ids, (DOMAINS, CAP))
    return jnp.where(slot_ids < NB + 4 * HB, fixed, picks).astype(jnp.int32)


def draw_tile_count(key, part):
    key = jax.random.fold_in(key, 31)
    first, second, third = jax.random.split(key, 3)
    base = NB + 4 * HB
    raw_ints = jax.random.randint(first, (DOMAINS,), 0, 65, dtype=jnp.int32)
    counts = base + (CAP - base) * raw_ints * raw_ints * raw_ints // 262144
    heavy = jax.random.randint(second, (), 0, DOMAINS, dtype=jnp.int32)
    light = (heavy + 1 + jax.random.randint(third, (), 0, DOMAINS - 1, dtype=jnp.int32)) % DOMAINS
    domain_ids = jnp.arange(DOMAINS, dtype=jnp.int32)
    counts = jnp.where(domain_ids == heavy, CAP, counts)
    counts = jnp.where(domain_ids == light, base, counts)
    return counts.astype(jnp.int32)


def set_ends(drawn, stream_key, least, high):
    index_at = [jax.random.randint(jax.random.fold_in(stream_key, axis), (), 0, length) for axis, length in enumerate(drawn.shape)]
    main_axis = drawn.shape.index(max(drawn.shape))
    beside = index_at[:main_axis] + [(index_at[main_axis] + 1) % drawn.shape[main_axis]] + index_at[main_axis + 1:]
    return drawn.at[tuple(index_at)].set(least).at[tuple(beside)].set(high)


def setup_inputs(seed: int = 0) -> dict:
    keys = jax.random.split(jax.random.key(seed), 8)
    return {
        "x_start": draw_x_start(jax.random.fold_in(keys[7], 71), 0),
        "p_start": draw_p_start(jax.random.fold_in(keys[7], 71), 0),
        "tiles": draw_tiles(jax.random.fold_in(keys[7], 71), 0),
        "tile_row": draw_tile_row(jax.random.fold_in(keys[7], 71), 0),
        "tile_col": draw_tile_col(jax.random.fold_in(keys[7], 71), 0),
        "tile_count": draw_tile_count(jax.random.fold_in(keys[7], 71), 0),
        "send_rows": set_ends(jax.random.randint(keys[6], (DOMAINS, 4, HALO), 0, NODES_DEV), jax.random.fold_in(keys[6], 1), 0, NODES_DEV - 1).astype(jnp.int32),
    }


RIDGE = 0.001

def highdot(left_mat, right_mat):
    return jnp.dot(left_mat, right_mat, precision=lax.Precision.HIGHEST)

def symmetric(matrix):
    return 0.5 * (matrix + matrix.T)

def ritz_coeffs(gram_mat, proj_mat):
    order = gram_mat.shape[0]
    identity = jnp.eye(order, dtype=jnp.float32)
    scaling = 1.0 / jnp.sqrt(jnp.diagonal(gram_mat) + 1e-06)
    scaled = gram_mat * scaling[:, None] * scaling[None, :] + RIDGE * identity
    factor = jnp.linalg.cholesky(scaled)
    inner = lax.linalg.triangular_solve(factor, proj_mat * scaling[:, None] * scaling[None, :], left_side=True, lower=True)
    reduced = symmetric(lax.linalg.triangular_solve(factor, inner.T, left_side=True, lower=True))
    radius = jnp.sqrt(jnp.sum(reduced * reduced)) + 1e-06
    shifted = identity - reduced / radius
    basis = factor.T[:, :K] / scaling[None, :K]
    for sweep in range(QSTEPS):
        basis = highdot(shifted, basis)
        small = jnp.linalg.cholesky(symmetric(highdot(basis.T, basis)))
        basis = lax.linalg.triangular_solve(small, basis.T, left_side=True, lower=True).T
    coeffs = lax.linalg.triangular_solve(factor, basis, left_side=True, lower=True, transpose_a=True)
    return coeffs * scaling[:, None]

def solve_theta(gram_xx, proj_xx):
    factor = jnp.linalg.cholesky(gram_xx)
    inner = lax.linalg.triangular_solve(factor, proj_xx, left_side=True, lower=True)
    return lax.linalg.triangular_solve(factor, inner, left_side=True, lower=True, transpose_a=True)

def apply_tiles(field, tiles, tile_row, tile_col, tile_count, send_rows):
    width = field.shape[1]
    halved = field.astype(jnp.bfloat16).reshape(N_REGION, N_DOM, NODES_DEV, width)
    row_lists = send_rows.reshape(N_REGION, N_DOM, 4, HALO)
    outbound = jax.vmap(jax.vmap(lambda values, picks: values[picks]))(halved, row_lists)
    from_left = jnp.roll(outbound[:, :, 0], 1, axis=1)
    from_right = jnp.roll(outbound[:, :, 1], -1, axis=1)
    nothing = jnp.zeros_like(outbound[:1, :, 2])
    from_below = jnp.concatenate([nothing, outbound[:-1, :, 2]], axis=0)
    from_above = jnp.concatenate([outbound[1:, :, 3], nothing], axis=0)
    extended = jnp.concatenate([halved, from_left, from_right, from_below, from_above], axis=2)
    extended = extended.reshape(DOMAINS, EXT_B, TB, width)

    def domain_product(packed):
        ext_dom, tile_dom, row_dom, col_dom, live_count = packed
        blocks = ext_dom[col_dom].astype(jnp.float32)
        partial_value = jnp.einsum('sij,sjc->sic', tile_dom.astype(jnp.float32), blocks, precision=lax.Precision.HIGHEST)
        active = jnp.arange(CAP) < live_count
        onehot = ((row_dom[None, :] == jnp.arange(NB)[:, None]) & active[None, :]).astype(jnp.float32)
        summed = jnp.einsum('bs,sic->bic', onehot, partial_value, precision=lax.Precision.HIGHEST)
        return summed.reshape(NODES_DEV, width)
    result = lax.map(domain_product, (extended, tiles, tile_row, tile_col, tile_count))
    return result.reshape(NODES, width)

def reference(x_start, p_start, tiles, tile_row, tile_col, tile_count, send_rows):
    vectors = x_start
    direction = p_start
    both = apply_tiles(jnp.concatenate([vectors, direction], axis=1), tiles, tile_row, tile_col, tile_count, send_rows)
    image_vec = both[:, :K]
    image_dir = both[:, K:]
    for iteration in range(ITERS):
        gram_xx = symmetric(highdot(vectors.T, vectors)) / NODES
        proj_xx = symmetric(highdot(vectors.T, image_vec)) / NODES
        ritz_vals = solve_theta(gram_xx, proj_xx)
        residual = image_vec - highdot(vectors, ritz_vals)
        twice = apply_tiles(image_vec, tiles, tile_row, tile_col, tile_count, send_rows)
        img_res = twice - highdot(image_vec, ritz_vals)
        pieces = [vectors, residual, direction]
        images = [image_vec, img_res, image_dir]
        gram_mat = symmetric(jnp.block([[highdot(first.T, second) for second in pieces] for first in pieces])) / NODES
        proj_mat = symmetric(jnp.block([[highdot(first.T, second) for second in images] for first in pieces])) / NODES
        coeffs = ritz_coeffs(gram_mat, proj_mat)
        coef_x = coeffs[:K]
        coef_r = coeffs[K:2 * K]
        coef_p = coeffs[2 * K:]
        new_dir = highdot(residual, coef_r) + highdot(direction, coef_p)
        new_vec = highdot(vectors, coef_x) + new_dir
        new_imgdir = highdot(img_res, coef_r) + highdot(image_dir, coef_p)
        image_vec = highdot(image_vec, coef_x) + new_imgdir
        image_dir = new_imgdir
        vectors = new_vec
        direction = new_dir
    return (vectors, direction)
```

```python
import jax
import jax.numpy as jnp
from jax import lax
from jax.experimental import pallas as pl
from jax.experimental.pallas import tpu as pltpu
from jax.sharding import PartitionSpec as P

K = 128
ITERS = 3
RIDGE = 0.001
NODES = 131072
ROWS = 1024
HALO = 512
CAP = 40
GROUP = 8
AXES = ("region", "dom")
F32 = jnp.float32
BF16 = jnp.bfloat16
SCALE = 1.0 / NODES
VMEM_LIMIT = 50 * 1024 * 1024


def dot(a, b):
    return jnp.dot(a, b, precision=lax.Precision.HIGHEST, preferred_element_type=F32)


def dot_tn(a, b):
    return lax.dot_general(
        a,
        b,
        (((0,), (0,)), ((), ())),
        precision=lax.Precision.HIGHEST,
        preferred_element_type=F32,
    )


def dot_nt(a, b):
    return lax.dot_general(
        a,
        b,
        (((1,), (1,)), ((), ())),
        precision=lax.Precision.HIGHEST,
        preferred_element_type=F32,
    )


def halves(m):
    high = m.astype(BF16)
    return high, (m - high.astype(F32)).astype(BF16)


def dot_split(a, b):
    a1, a2 = halves(a)
    b1, b2 = halves(b)
    return jnp.dot(
        jnp.concatenate([a1, a1, a2], axis=1),
        jnp.concatenate([b1, b2, b1], axis=0),
        preferred_element_type=F32,
    )


def dot_split_tn(a, b):
    a1, a2 = halves(a)
    b1, b2 = halves(b)
    return lax.dot_general(
        jnp.concatenate([a1, a1, a2], axis=0),
        jnp.concatenate([b1, b2, b1], axis=0),
        (((0,), (0,)), ((), ())),
        preferred_element_type=F32,
    )


def sym(m):
    return 0.5 * (m + m.T)


def eye():
    row = lax.broadcasted_iota(jnp.int32, (K, K), 0)
    col = lax.broadcasted_iota(jnp.int32, (K, K), 1)
    return jnp.where(row == col, 1.0, 0.0).astype(F32)


def inv_scales(m, ident):
    d = m * ident
    col = 1.0 / jnp.sqrt(jnp.sum(d, axis=1, keepdims=True) + 1e-06)
    row = 1.0 / jnp.sqrt(jnp.sum(d, axis=0, keepdims=True) + 1e-06)
    return col, row


def eliminate(systems, ahead=True):
    sub = lax.broadcasted_iota(jnp.int32, (8, K), 0)

    def row(x, t):
        return jnp.broadcast_to(x[t : t + 1, :], (8, K))

    def lane(x, j):
        return jnp.broadcast_to(x[:, j : j + 1], (8, K))

    def total(terms):
        while len(terms) > 1:
            terms = [terms[i] + terms[i + 1] for i in range(0, len(terms), 2)]
        return terms[0]

    def swap(x):
        return jnp.where(sub % 2 == 0, pltpu.roll(x, 7, 0), pltpu.roll(x, 1, 0))

    kept = [None] * len(systems)
    for p in range(K // 8):
        base = 8 * p
        for n, (a_ref, b_ref, full) in enumerate(systems):
            pa = a_ref[base : base + 8, :]
            pb = b_ref[base : base + 8, :]
            cols = kept[n]
            if cols is None:
                cols = [lane(pa, base + t) for t in range(8)]
            follow = [lane(pa, base + 8 + t) for t in range(8)] if ahead and p + 1 < K // 8 else []
            diag = jnp.zeros((8, K), F32)
            off = jnp.zeros((8, K), F32)
            low = pb
            for t in range(0, 8, 2):
                c0, c1 = cols[t], cols[t + 1]
                a, b, d = row(c0, t), row(c1, t), row(c1, t + 1)
                det = a * d - b * b
                rdet = 1.0 / det
                outside = (sub < t) | (sub > t + 1)
                m0 = jnp.where(outside, c0 * d - c1 * b, 0.0) * rdet
                m1 = jnp.where(outside, c1 * a - c0 * b, 0.0) * rdet
                for u in range(t + 2, 8):
                    cols[u] = cols[u] - (m0 * row(cols[u], t) + m1 * row(cols[u], t + 1))
                if not full:
                    ra = 1.0 / a
                    first, second = row(pb, t), row(pb, t + 1)
                    low = jnp.where(sub == t, first * lax.rsqrt(a), low)
                    low = jnp.where(
                        sub == t + 1, (second - first * (b * ra)) * lax.rsqrt(det * ra), low
                    )
                diag = jnp.where(sub == t, d * rdet, jnp.where(sub == t + 1, a * rdet, diag))
                off = jnp.where(outside, off, -b * rdet)
                pa = pa - (m0 * row(pa, t) + m1 * row(pa, t + 1))
                pb = pb - (m0 * row(pb, t) + m1 * row(pb, t + 1))
                follow = [f - (m0 * row(f, t) + m1 * row(f, t + 1)) for f in follow]
            pa = pa * diag + swap(pa) * off
            pb = pb * diag + swap(pb) * off
            follow = [f * diag + swap(f) * off for f in follow]
            ra = [row(pa, t) for t in range(8)]
            rb = [row(pb, t) for t in range(8)]
            kept[n] = None
            for i in range(K // 8):
                if i == p or (i < p and not full):
                    continue
                blk = a_ref[8 * i : 8 * i + 8, :]
                rhs = b_ref[8 * i : 8 * i + 8, :]
                c = [lane(blk, base + t) for t in range(8)]
                if follow and i == p + 1:
                    kept[n] = [
                        lane(blk, base + 8 + u) - total([c[t] * row(follow[u], t) for t in range(8)])
                        for u in range(8)
                    ]
                a_ref[8 * i : 8 * i + 8, :] = blk - total([c[t] * ra[t] for t in range(8)])
                b_ref[8 * i : 8 * i + 8, :] = rhs - total([c[t] * rb[t] for t in range(8)])
            if full:
                a_ref[base : base + 8, :] = pa
                b_ref[base : base + 8, :] = pb
            else:
                b_ref[base : base + 8, :] = low


def gather_rows(field, idx_ref, outs):
    lanes = lax.broadcasted_iota(jnp.int32, (HALO, K), 1)
    for d, out in enumerate(outs):
        picks = idx_ref[d * HALO : (d + 1) * HALO, :]
        hot = jnp.concatenate(
            [
                jnp.where(picks == lanes + K * c, 1.0, 0.0).astype(BF16)
                for c in range(ROWS // K)
            ],
            axis=1,
        )
        out[...] = jnp.dot(hot, field, preferred_element_type=F32).astype(BF16)


def apply_operator(own, halos, tiles_ref, row_ref, col_ref, count_ref, ext_ref, acc_ref):
    ext_ref[0:ROWS, :] = own
    for i, h in enumerate(halos):
        ext_ref[ROWS + i * HALO : ROWS + (i + 1) * HALO, :] = h[...]
    acc_ref[...] = jnp.zeros_like(acc_ref)
    count = count_ref[0]

    def group(g, carry):
        parts = []
        for j in range(GROUP):
            s = g * GROUP + j
            col = pl.multiple_of(col_ref[s] * K, K)
            prod = jnp.dot(tiles_ref[s], ext_ref[pl.ds(col, K), :], preferred_element_type=F32)
            parts.append(jnp.where(s < count, prod, 0.0))
        for j in range(GROUP):
            row = pl.multiple_of(row_ref[g * GROUP + j] * K, K)
            acc_ref[pl.ds(row, K), :] += parts[j]
        return carry

    lax.fori_loop(0, CAP // GROUP, group, 0)


def first_gather_kernel(x_ref, p_ref, idx_ref, *outs):
    both = jnp.concatenate([x_ref[...], p_ref[...]], axis=1).astype(BF16)
    gather_rows(both, idx_ref, outs)


def first_operator_kernel(
    x_ref, p_ref, h0, h1, h2, h3, tiles_ref, idx_ref, row_ref, col_ref, count_ref,
    ax_ref, ap_ref, o0, o1, o2, o3, ext_ref, acc_ref,
):
    own = jnp.concatenate([x_ref[...], p_ref[...]], axis=1).astype(BF16)
    apply_operator(
        own, (h0, h1, h2, h3), tiles_ref, row_ref, col_ref, count_ref, ext_ref, acc_ref
    )
    ax = acc_ref[:, :K]
    ax_ref[...] = ax
    ap_ref[...] = acc_ref[:, K:]
    gather_rows(ax.astype(BF16), idx_ref, (o0, o1, o2, o3))


def first_side_kernel(x_ref, p_ref, ax_ref, ap_ref, out_ref):
    x, p, ax, ap = x_ref[...], p_ref[...], ax_ref[...], ap_ref[...]
    wide = dot_split_tn(ax, jnp.concatenate([ax, ap], axis=1))
    out_ref[0:K, :] = wide[:, :K]
    out_ref[K : 2 * K, :] = wide[:, K:]
    right = jnp.concatenate([x, p, ax, ap], axis=1)
    top = dot_split_tn(x, right)
    low = dot_split_tn(p, right[:, K:])
    parts = (
        top[:, 0:K],
        top[:, K : 2 * K],
        low[:, 0:K],
        top[:, 2 * K : 3 * K],
        top[:, 3 * K :],
        low[:, K : 2 * K],
        low[:, 2 * K :],
    )
    for i, part in enumerate(parts):
        out_ref[(2 + i) * K : (3 + i) * K, :] = part


def combine(first, second, third, d_ref):
    return dot_split(jnp.concatenate([first, second, third], axis=1), d_ref[...])


def side_kernel(x_ref, p_ref, ax_ref, nax_ref, nap_ref, d_ref, nx_ref, np_ref, out_ref):
    new = combine(x_ref[...], ax_ref[...], p_ref[...], d_ref)
    np_ref[...] = new[:, :K]
    nx_ref[...] = new[:, K:]
    nax = nax_ref[...]
    wide = dot_split_tn(nax, jnp.concatenate([nax, nap_ref[...]], axis=1))
    out_ref[0:K, :] = wide[:, :K]
    out_ref[K : 2 * K, :] = wide[:, K:]


def final_kernel(x_ref, p_ref, ax_ref, d_ref, nx_ref, np_ref):
    new = combine(x_ref[...], ax_ref[...], p_ref[...], d_ref)
    np_ref[...] = new[:, :K]
    nx_ref[...] = new[:, K:]


def update_kernel(ax_ref, q_ref, ap_ref, d_ref, idx_ref, nax_ref, nap_ref, o0, o1, o2, o3):
    new = combine(ax_ref[...], q_ref[...], ap_ref[...], d_ref)
    nap_ref[...] = new[:, :K]
    new_ax = new[:, K:]
    nax_ref[...] = new_ax
    gather_rows(new_ax.astype(BF16), idx_ref, (o0, o1, o2, o3))


def operator_kernel(
    x_ref, ax_ref, p_ref, h0, h1, h2, h3, tiles_ref, side_ref, row_ref, col_ref, count_ref, core_ref,
    q_ref, keep_ref, give_ref, ext_ref, acc_ref, pay_ref,
):
    ax = ax_ref[...]
    apply_operator(
        ax.astype(BF16), (h0, h1, h2, h3), tiles_ref, row_ref, col_ref, count_ref, ext_ref, acc_ref
    )
    q = acc_ref[...]
    q_ref[...] = q
    wide = dot_split_tn(q, jnp.concatenate([x_ref[...], ax, p_ref[...]], axis=1))
    for i in range(3):
        pay_ref[i * K : (i + 1) * K, :] = wide[:, i * K : (i + 1) * K]
    pay_ref[3 * K :, :] = side_ref[...]
    half = pay_ref.shape[0] // 2
    core = core_ref[0]
    keep_ref[...] = pay_ref[pl.ds(pl.multiple_of(core * half, 8), half), :]
    give_ref[...] = pay_ref[pl.ds(pl.multiple_of((1 - core) * half, 8), half), :]


KNOWN = ("xx", "xp", "pp", "k", "xap", "pax", "pap")
STAGE1 = ("theta", "a1", "u12", "s22")
STAGE2 = (
    "gxr", "gpr", "v13", "thk", "zr1", "kth", "paxth", "thxap", "a2", "v23", "a21",
)
STAGE3 = ("n33", "n31", "n32", "m11", "m12", "m22")
ALL_STAGES = (KNOWN, STAGE1, STAGE2, STAGE3)


def reader(names, refs):
    place = {name: (ref, i) for group, ref in zip(names, refs) for i, name in enumerate(group)}

    def get(name):
        ref, i = place[name]
        return ref[i]

    return get


def put(names, ref, values):
    for i, name in enumerate(names):
        ref[i] = values[name]


def join_halves(own_ref, other_ref, core_ref, pay_ref):
    half = own_ref.shape[0]
    core = core_ref[0]
    pay_ref[pl.ds(pl.multiple_of(core * half, 8), half), :] = own_ref[...]
    pay_ref[pl.ds(pl.multiple_of((1 - core) * half, 8), half), :] = other_ref[...]


def stage1(get, sa, sb, sc, sd):
    ident = eye()
    xx, pp = get("xx"), get("pp")
    ex_c, ex_r = inv_scales(xx, ident)
    ep_c, ep_r = inv_scales(pp, ident)
    sa[...] = xx * ex_c * ex_r + RIDGE * ident
    sb[...] = ident
    sc[...] = xx
    sd[...] = sym(get("k"))
    eliminate([(sa, sb, False), (sc, sd, True)], False)
    a1 = sb[...] * ex_r
    u12 = dot(a1, get("xp")) * ep_r
    s22 = pp * ep_c * ep_r + RIDGE * ident - dot_tn(u12, u12)
    return {"theta": sd[...], "a1": a1, "u12": u12, "s22": s22}


def stage2(get, sa, sb):
    ident = eye()
    sa[...] = get("s22")
    sb[...] = ident
    theta, a1, u12, k, pax = get("theta"), get("a1"), get("u12"), get("k"), get("pax")
    gxr = k - dot(get("xx"), theta)
    gpr = pax - dot_tn(get("xp"), theta)
    v13 = dot(a1, gxr)
    thk = dot_tn(theta, k)
    out = {
        "gxr": gxr,
        "gpr": gpr,
        "v13": v13,
        "thk": thk,
        "zr1": thk + dot_tn(gxr, theta),
        "kth": dot(k, theta),
        "paxth": dot(pax, theta),
        "thxap": dot_tn(theta, get("xap")),
    }
    low = dot_tn(u12, jnp.concatenate([v13, a1], axis=1))
    ep_r = inv_scales(get("pp"), ident)[1]
    eliminate([(sa, sb, False)])
    y2 = sb[...]
    out["a2"] = y2 * ep_r
    out["v23"] = dot(y2, gpr * inv_scales(get("pp"), ident)[0] - low[:, :K])
    out["a21"] = -dot(y2, low[:, K:])
    return out


def stage3(get):
    a1, a2, a21, v13, v23 = (get(n) for n in ("a1", "a2", "a21", "v13", "v23"))
    one = dot_tn(v13, jnp.concatenate([v13, a1], axis=1))
    two = dot_tn(v23, jnp.concatenate([v23, a21, a2], axis=1))
    h12 = 0.5 * (get("xap") + get("pax").T)
    left = jnp.concatenate(
        [
            jnp.concatenate([a1, jnp.zeros_like(a1)], axis=1),
            jnp.concatenate([a21, a2], axis=1),
        ],
        axis=0,
    )
    mid = jnp.concatenate(
        [
            jnp.concatenate([sym(get("k")), h12], axis=1),
            jnp.concatenate([h12.T, sym(get("pap"))], axis=1),
        ],
        axis=0,
    )
    mpp = dot_nt(dot(left, mid), left)
    return {
        "n33": one[:, :K] + two[:, :K],
        "n31": one[:, K:] + two[:, K : 2 * K],
        "n32": two[:, 2 * K :],
        "m11": mpp[:K, :K],
        "m12": mpp[:K, K:],
        "m22": mpp[K:, K:],
    }


def first_prepare_kernel(
    own_ref, other_ref, core_ref, r0, r1, r2, r3, new_ref, pay_ref, sa, sb, sc, sd
):
    join_halves(own_ref, other_ref, core_ref, pay_ref)
    new_ref[...] = pay_ref[0 : 5 * K, :]
    for i in range(7):
        r0[i] = pay_ref[(5 + i) * K : (6 + i) * K, :] * SCALE
    get = reader(ALL_STAGES, (r0, r1, r2, r3))
    put(STAGE1, r1, stage1(get, sa, sb, sc, sd))
    put(STAGE2, r2, stage2(get, sa, sb))
    put(STAGE3, r3, stage3(get))


def known_kernel(g_ref, h_ref, c_ref, r0):
    c = c_ref[...]
    top = jnp.concatenate([c[:K], jnp.zeros((K, K), F32)], axis=1)
    both = jnp.concatenate([top, jnp.concatenate([c[K:], c[K:]], axis=1)], axis=0)
    gg = dot_tn(both, dot(g_ref[...], both))
    hh = dot_tn(both, dot(h_ref[...], both))
    values = (
        gg[:K, :K],
        gg[:K, K:],
        gg[K:, K:],
        hh[:K, :K],
        hh[:K, K:],
        hh[K:, :K],
        hh[K:, K:],
    )
    put(KNOWN, r0, dict(zip(KNOWN, values)))


def stage1_kernel(r0, after_ref, r1, sa, sb, sc, sd):
    put(STAGE1, r1, stage1(reader(ALL_STAGES[:1], (r0,)), sa, sb, sc, sd))


def stage2_kernel(r0, r1, after_ref, r2, sa, sb):
    put(STAGE2, r2, stage2(reader(ALL_STAGES[:2], (r0, r1)), sa, sb))


def stage3_kernel(r0, r1, r2, after_ref, r3):
    put(STAGE3, r3, stage3(reader(ALL_STAGES[:3], (r0, r1, r2))))


def fill(ref, rows):
    for i, line in enumerate(rows):
        for j, value in enumerate(line):
            ref[i * K : (i + 1) * K, j * K : (j + 1) * K] = value


def solve(pay_ref, get, c_ref, d_ref, g_ref, h_ref, le, hs, sa, sb):
    qx, qax, qp, axax, axap = (pay_ref[i * K : (i + 1) * K, :] * SCALE for i in range(5))
    ident = eye()
    theta = get("theta")
    grr = sym(axax - get("zr1"))
    er_c, er_r = inv_scales(grr, ident)
    sa[...] = (grr - get("n33")) * er_c * er_r + RIDGE * ident
    sb[...] = ident
    xq = qx.T
    hxr = xq - get("kth")
    hrx = axax - get("thk")
    hrp = axap - get("thxap")
    hpr = qp.T - get("paxth")
    hrr = qax.T - dot_tn(theta, xq) - dot(hrx, theta)
    if g_ref is not None:
        xp, gxr, gpr = get("xp"), get("gxr"), get("gpr")
        fill(g_ref, ((get("xx"), xp, gxr), (xp.T, get("pp"), gpr), (gxr.T, gpr.T, grr)))
        fill(
            h_ref,
            ((get("k"), get("xap"), hxr), (get("pax"), get("pap"), hpr), (hrx, hrp, hrr)),
        )
    h13 = 0.5 * (hxr + hrx.T)
    h23 = 0.5 * (hpr + hrp.T)
    h12 = 0.5 * (get("xap") + get("pax").T)
    zero = jnp.zeros((K, K), F32)
    fill(
        hs,
        (
            (sym(get("k")), h12, h13),
            (h12.T, sym(get("pap")), h23),
            (h13.T, h23.T, sym(hrr)),
        ),
    )
    eliminate([(sa, sb, False)])
    a3 = sb[...] * er_r
    both = -dot(a3, jnp.concatenate([get("n31"), get("n32")], axis=1))
    fill(le, ((get("a1"), zero, zero), (get("a21"), get("a2"), zero), (both[:, :K], both[:, K:], a3)))
    last = dot(le[...], dot_nt(hs[...], le[2 * K :, :]))
    m13, m23, m33 = last[:K], last[K : 2 * K], last[2 * K :]
    m11, m12, m22 = get("m11"), get("m12"), get("m22")
    square = (
        m11 * m11 + m22 * m22 + m33 * m33 + 2.0 * (m12 * m12 + m13 * m13 + m23 * m23)
    )
    scale = 1.0 / (jnp.sqrt(jnp.sum(square, keepdims=True)) + 1e-06)
    m11, m12, m13, m22, m23, m33 = (x * scale for x in (m11, m12, m13, m22, m23, m33))
    fill(hs, ((m11, m12, m13), (m12.T, m22, m23), (m13.T, m23.T, m33)))
    m = hs[...]
    start = jnp.concatenate([ident, zero, zero], axis=0)
    basis = start - m[:, :K]
    basis = basis - dot(m, basis)
    basis = basis - dot(m, basis)
    sa[...] = dot_tn(basis, basis)
    sb[...] = ident
    raw = dot_tn(le[...], basis)
    raw = jnp.concatenate([raw, dot(theta, raw[2 * K :])], axis=0)
    eliminate([(sa, sb, False)])
    c = dot_nt(raw, sb[...])
    cx, cp, cr, low = c[:K], c[K : 2 * K], c[2 * K : 3 * K], -c[3 * K :]
    if c_ref is not None:
        c_ref[...] = c[: 3 * K]
    fill(d_ref, ((low, low + cx), (cr, cr), (cp, cp)))


def first_solve_kernel(new_ref, r0, r1, r2, r3, c_ref, d_ref, g_ref, h_ref, le, hs, sa, sb):
    get = reader(ALL_STAGES, (r0, r1, r2, r3))
    solve(new_ref, get, c_ref, d_ref, g_ref, h_ref, le, hs, sa, sb)


def solve_kernel(
    own_ref, other_ref, core_ref, r0, r1, r2, r3, c_ref, d_ref, g_ref, h_ref, pay_ref, le, hs, sa, sb
):
    join_halves(own_ref, other_ref, core_ref, pay_ref)
    get = reader(ALL_STAGES, (r0, r1, r2, r3))
    solve(pay_ref, get, c_ref, d_ref, g_ref, h_ref, le, hs, sa, sb)


def last_solve_kernel(
    own_ref, other_ref, core_ref, r0, r1, r2, r3, d_ref, pay_ref, le, hs, sa, sb
):
    join_halves(own_ref, other_ref, core_ref, pay_ref)
    get = reader(ALL_STAGES, (r0, r1, r2, r3))
    solve(pay_ref, get, None, d_ref, None, None, le, hs, sa, sb)


VM = pl.BlockSpec(memory_space=pltpu.VMEM)
SM = pl.BlockSpec(memory_space=pltpu.SMEM)


def shape(*dims, dtype=F32):
    return jax.ShapeDtypeStruct(dims, dtype)


def call(kernel, ins, outs, scratch, name, us=3):
    arrays = [a for a, _ in ins]
    return pl.pallas_call(
        kernel,
        out_shape=tuple(outs),
        in_specs=[s for _, s in ins],
        out_specs=tuple(VM for _ in outs),
        scratch_shapes=scratch,
        compiler_params=pltpu.CompilerParams(vmem_limit_bytes=VMEM_LIMIT),
        cost_estimate=pl.CostEstimate(
            flops=us * 10**9, bytes_accessed=0, transcendentals=0
        ),
        name=name,
    )(*arrays)


def v(*arrays):
    return [(a, VM) for a in arrays]


def s(*arrays):
    return [(a, SM) for a in arrays]


def coords(i):
    region, dom = divmod(i, 8)
    return [region // 4, region % 4, dom // 2, dom % 2]


def index(z, y, x, core):
    return ((z * 4 + y) * 4 + x) * 2 + core


def flip(dim, kind):
    out = []
    for i in range(128):
        at = coords(i)
        if dim == 3 or kind == 0:
            at[dim] ^= 1
        else:
            at[dim] = {1: 2, 2: 1, 3: 0, 0: 3}[at[dim]]
        out.append((i, index(*at)))
    return out


def after(first, second):
    second = dict(second)
    return [(i, second[j]) for i, j in first]


def send(x, perm):
    return lax.ppermute(x, AXES, perm)


def all_sum(keep, give):
    y = keep + send(give, flip(3, 0))
    third = y.shape[0] // 24 * 8
    parts = [y[:third], y[third : 2 * third], y[2 * third :]]
    for kind in (0, 1):
        for r in range(3):
            parts = [p + send(p, flip((2 - r - i) % 3, kind)) for i, p in enumerate(parts)]
    y = jnp.concatenate(parts, axis=0)
    return y, send(y, flip(3, 0))


def all_sum_beside(keep, give, stages):
    y = keep + send(give, flip(3, 0))
    done = ()
    rounds = (((2, 0), (1, 0)), ((0, 0), (2, 1)), ((1, 1), (0, 1)))
    for (one, two), stage in zip(rounds, stages):
        fa, fb = flip(*one), flip(*two)
        ga, gb, gab = send(y, fa), send(y, fb), send(y, after(fa, fb))
        done = done + (stage(y[:8], done),)
        y = (y + ga) + (gb + gab)
    return y, send(y, flip(3, 0)), done


def halo(outs):
    n_dom, n_region = 8, 16
    up = [(i, (i + 1) % n_dom) for i in range(n_dom)]
    down = [(j, i) for i, j in up]
    north = [(i, i + 1) for i in range(n_region - 1)]
    south = [(j, i) for i, j in north]
    return (
        lax.ppermute(outs[0], "dom", up),
        lax.ppermute(outs[1], "dom", down),
        lax.ppermute(outs[2], "region", north),
        lax.ppermute(outs[3], "region", south),
    )


def body(x, p, tiles, tile_row, tile_col, tile_count, send_rows):
    tiles = tiles[0]
    where = s(tile_row[0], tile_col[0], tile_count)
    core = jnp.reshape(lax.axis_index("dom") % 2, (1,)).astype(jnp.int32)
    idx = jnp.broadcast_to(send_rows.reshape(4 * HALO, 1), (4 * HALO, K))
    outs = [shape(HALO, K, dtype=BF16)] * 4
    wide = [shape(HALO, 2 * K, dtype=BF16)] * 4
    field = shape(ROWS, K)
    square = pltpu.VMEM((K, K), F32)
    big = pltpu.VMEM((3 * K, 3 * K), F32)

    sent = call(first_gather_kernel, v(x, p, idx), wide, [], "first_gather")
    got = halo(sent)
    ax, ap, *sent = call(
        first_operator_kernel,
        v(x, p, *got, tiles, idx) + where,
        [field, field] + outs,
        [pltpu.VMEM((3 * ROWS, 2 * K), BF16), pltpu.VMEM((ROWS, 2 * K), F32)],
        "first_operator",
    )
    sizes = [shape(len(names), K, K) for names in ALL_STAGES]
    for it in range(ITERS):
        got = halo(sent)
        if it == 0:
            (side,) = call(
                first_side_kernel, v(x, p, ax, ap), [shape(9 * K, K)], [], "first_side", 2
            )
        else:
            x, p, side = call(
                side_kernel,
                v(x, p, old_ax, ax, ap, d),
                [field, field, shape(2 * K, K)],
                [],
                "side",
                2,
            )
            (r0,) = call(known_kernel, v(g, h, c), sizes[:1], [], "known", 4)
        pay = 12 * K if it == 0 else 5 * K
        q, keep, give = call(
            operator_kernel,
            v(x, ax, p, *got, tiles, side) + where + s(core),
            [field, shape(pay // 2, K), shape(pay // 2, K)],
            [
                pltpu.VMEM((3 * ROWS, K), BF16),
                pltpu.VMEM((ROWS, K), F32),
                pltpu.VMEM((pay, K), F32),
            ],
            "operator",
        )
        coef = [shape(3 * K, K), shape(3 * K, 2 * K)]
        gram = [shape(3 * K, 3 * K)] * 2
        scratch = [big, big, square, square]
        pay_scratch = [pltpu.VMEM((pay, K), F32)]
        if it == 0:
            own, other = all_sum(keep, give)
            *st, new = call(
                first_prepare_kernel,
                v(own, other) + s(core),
                sizes + [shape(5 * K, K)],
                pay_scratch + [square] * 4,
                "first_prepare",
            )
            c, d, g, h = call(first_solve_kernel, v(new, *st), coef + gram, scratch, "first_solve")
        else:

            def one(y, done):
                return call(stage1_kernel, v(r0, y), sizes[1:2], [square] * 4, "stage1", 7)[0]

            def two(y, done):
                return call(stage2_kernel, v(r0, *done, y), sizes[2:3], [square] * 2, "stage2", 5)[0]

            def three(y, done):
                return call(stage3_kernel, v(r0, *done, y), sizes[3:], [], "stage3", 3)[0]

            own, other, done = all_sum_beside(keep, give, (one, two, three))
            last = it + 1 == ITERS
            res = call(
                last_solve_kernel if last else solve_kernel,
                v(own, other) + s(core) + v(r0, *done),
                coef[1:] if last else coef + gram,
                pay_scratch + scratch,
                "last_solve" if last else "solve",
            )
            c, d, g, h = (None, *res, None, None) if last else res
        if it + 1 < ITERS:
            old_ax = ax
            ax, ap, *sent = call(
                update_kernel, v(ax, q, ap, d, idx), [field, field] + outs, [], "update"
            )
        else:
            x, p = call(final_kernel, v(x, p, ax, d), [field, field], [], "final")
    return x, p


def solution(mesh):
    in_specs = (
        P(AXES, None),
        P(AXES, None),
        P(AXES, None, None, None),
        P(AXES, None),
        P(AXES, None),
        P(AXES),
        P(AXES, None, None),
    )
    out_specs = (P(AXES, None), P(AXES, None))
    return jax.shard_map(body, mesh=mesh, in_specs=in_specs, out_specs=out_specs, check_vma=False)
```

```python
import jax
import jax.numpy as jnp
from jax import lax
from jax.experimental import pallas as pl
from jax.experimental.pallas import tpu as pltpu
from jax.sharding import PartitionSpec as P

K = 128
ITERS = 3
RIDGE = 0.001
NODES = 131072
ROWS = 1024
HALO = 512
CAP = 40
GROUP = 8
AXES = ("region", "dom")
F32 = jnp.float32
BF16 = jnp.bfloat16
SCALE = 1.0 / NODES
VMEM_LIMIT = 40 * 1024 * 1024


def dot(a, b):
    return jnp.dot(a, b, precision=lax.Precision.HIGHEST, preferred_element_type=F32)


def dot_tn(a, b):
    return lax.dot_general(
        a,
        b,
        (((0,), (0,)), ((), ())),
        precision=lax.Precision.HIGHEST,
        preferred_element_type=F32,
    )


def dot_nt(a, b):
    return lax.dot_general(
        a,
        b,
        (((1,), (1,)), ((), ())),
        precision=lax.Precision.HIGHEST,
        preferred_element_type=F32,
    )


def halves(m):
    high = m.astype(BF16)
    return high, (m - high.astype(F32)).astype(BF16)


def dot_split(a, b):
    a1, a2 = halves(a)
    b1, b2 = halves(b)
    return jnp.dot(
        jnp.concatenate([a1, a1, a2], axis=1),
        jnp.concatenate([b1, b2, b1], axis=0),
        preferred_element_type=F32,
    )


def dot_split_tn(a, b):
    a1, a2 = halves(a)
    b1, b2 = halves(b)
    return lax.dot_general(
        jnp.concatenate([a1, a1, a2], axis=0),
        jnp.concatenate([b1, b2, b1], axis=0),
        (((0,), (0,)), ((), ())),
        preferred_element_type=F32,
    )


def sym(m):
    return 0.5 * (m + m.T)


def eye():
    row = lax.broadcasted_iota(jnp.int32, (K, K), 0)
    col = lax.broadcasted_iota(jnp.int32, (K, K), 1)
    return jnp.where(row == col, 1.0, 0.0).astype(F32)


def inv_scales(m, ident):
    d = m * ident
    col = 1.0 / jnp.sqrt(jnp.sum(d, axis=1, keepdims=True) + 1e-06)
    row = 1.0 / jnp.sqrt(jnp.sum(d, axis=0, keepdims=True) + 1e-06)
    return col, row


def eliminate(systems, ahead=True):
    sub = lax.broadcasted_iota(jnp.int32, (8, K), 0)

    def row(x, t):
        return jnp.broadcast_to(x[t : t + 1, :], (8, K))

    def lane(x, j):
        return jnp.broadcast_to(x[:, j : j + 1], (8, K))

    def total(terms):
        while len(terms) > 1:
            terms = [terms[i] + terms[i + 1] for i in range(0, len(terms), 2)]
        return terms[0]

    def swap(x):
        return jnp.where(sub % 2 == 0, pltpu.roll(x, 7, 0), pltpu.roll(x, 1, 0))

    kept = [None] * len(systems)
    for p in range(K // 8):
        base = 8 * p
        for n, (a_ref, b_ref, full) in enumerate(systems):
            pa = a_ref[base : base + 8, :]
            pb = b_ref[base : base + 8, :]
            cols = kept[n]
            if cols is None:
                cols = [lane(pa, base + t) for t in range(8)]
            follow = [lane(pa, base + 8 + t) for t in range(8)] if ahead and p + 1 < K // 8 else []
            diag = jnp.zeros((8, K), F32)
            off = jnp.zeros((8, K), F32)
            low = pb
            for t in range(0, 8, 2):
                c0, c1 = cols[t], cols[t + 1]
                a, b, d = row(c0, t), row(c1, t), row(c1, t + 1)
                det = a * d - b * b
                rdet = 1.0 / det
                outside = (sub < t) | (sub > t + 1)
                m0 = jnp.where(outside, c0 * d - c1 * b, 0.0) * rdet
                m1 = jnp.where(outside, c1 * a - c0 * b, 0.0) * rdet
                for u in range(t + 2, 8):
                    cols[u] = cols[u] - (m0 * row(cols[u], t) + m1 * row(cols[u], t + 1))
                if not full:
                    ra = 1.0 / a
                    first, second = row(pb, t), row(pb, t + 1)
                    low = jnp.where(sub == t, first * lax.rsqrt(a), low)
                    low = jnp.where(
                        sub == t + 1, (second - first * (b * ra)) * lax.rsqrt(det * ra), low
                    )
                diag = jnp.where(sub == t, d * rdet, jnp.where(sub == t + 1, a * rdet, diag))
                off = jnp.where(outside, off, -b * rdet)
                pa = pa - (m0 * row(pa, t) + m1 * row(pa, t + 1))
                pb = pb - (m0 * row(pb, t) + m1 * row(pb, t + 1))
                follow = [f - (m0 * row(f, t) + m1 * row(f, t + 1)) for f in follow]
            pa = pa * diag + swap(pa) * off
            pb = pb * diag + swap(pb) * off
            follow = [f * diag + swap(f) * off for f in follow]
            ra = [row(pa, t) for t in range(8)]
            rb = [row(pb, t) for t in range(8)]
            kept[n] = None
            for i in range(K // 8):
                if i == p or (i < p and not full):
                    continue
                blk = a_ref[8 * i : 8 * i + 8, :]
                rhs = b_ref[8 * i : 8 * i + 8, :]
                c = [lane(blk, base + t) for t in range(8)]
                if follow and i == p + 1:
                    kept[n] = [
                        lane(blk, base + 8 + u) - total([c[t] * row(follow[u], t) for t in range(8)])
                        for u in range(8)
                    ]
                a_ref[8 * i : 8 * i + 8, :] = blk - total([c[t] * ra[t] for t in range(8)])
                b_ref[8 * i : 8 * i + 8, :] = rhs - total([c[t] * rb[t] for t in range(8)])
            if full:
                a_ref[base : base + 8, :] = pa
                b_ref[base : base + 8, :] = pb
            else:
                b_ref[base : base + 8, :] = low


def one_hot(picks):
    lanes = lax.broadcasted_iota(jnp.int32, (HALO, K), 1)
    return jnp.concatenate(
        [jnp.where(picks == lanes + K * c, 1.0, 0.0).astype(BF16) for c in range(ROWS // K)],
        axis=1,
    )


def gather_rows(field, idx_ref, outs):
    for d, out in enumerate(outs):
        hot = one_hot(idx_ref[d * HALO : (d + 1) * HALO, :])
        out[...] = jnp.dot(hot, field, preferred_element_type=F32).astype(BF16)


def hot_kernel(idx_ref, hot_ref):
    for d in range(4):
        rows = slice(d * HALO, (d + 1) * HALO)
        hot_ref[rows, :] = one_hot(idx_ref[rows, :])


def apply_operator(own, halos, tiles_ref, row_ref, col_ref, count_ref, ext_ref, acc_ref):
    ext_ref[0:ROWS, :] = own
    for i, h in enumerate(halos):
        ext_ref[ROWS + i * HALO : ROWS + (i + 1) * HALO, :] = h[...]
    acc_ref[...] = jnp.zeros_like(acc_ref)
    count = count_ref[0]

    def group(g, carry):
        parts = []
        for j in range(GROUP):
            s = g * GROUP + j
            col = pl.multiple_of(col_ref[s] * K, K)
            prod = jnp.dot(tiles_ref[s], ext_ref[pl.ds(col, K), :], preferred_element_type=F32)
            parts.append(jnp.where(s < count, prod, 0.0))
        for j in range(GROUP):
            row = pl.multiple_of(row_ref[g * GROUP + j] * K, K)
            acc_ref[pl.ds(row, K), :] += parts[j]
        return carry

    lax.fori_loop(0, CAP // GROUP, group, 0)


def first_gather_kernel(x_ref, p_ref, idx_ref, *outs):
    both = jnp.concatenate([x_ref[...], p_ref[...]], axis=1).astype(BF16)
    gather_rows(both, idx_ref, outs)


def first_operator_kernel(
    x_ref, p_ref, h0, h1, h2, h3, tiles_ref, idx_ref, row_ref, col_ref, count_ref,
    ax_ref, ap_ref, o0, o1, o2, o3, ext_ref, acc_ref,
):
    own = jnp.concatenate([x_ref[...], p_ref[...]], axis=1).astype(BF16)
    apply_operator(
        own, (h0, h1, h2, h3), tiles_ref, row_ref, col_ref, count_ref, ext_ref, acc_ref
    )
    ax = acc_ref[:, :K]
    ax_ref[...] = ax
    ap_ref[...] = acc_ref[:, K:]
    gather_rows(ax.astype(BF16), idx_ref, (o0, o1, o2, o3))


def first_side_kernel(x_ref, p_ref, ax_ref, ap_ref, out_ref):
    x, p, ax, ap = x_ref[...], p_ref[...], ax_ref[...], ap_ref[...]
    wide = dot_split_tn(ax, jnp.concatenate([ax, ap], axis=1))
    out_ref[0:K, :] = wide[:, :K]
    out_ref[K : 2 * K, :] = wide[:, K:]
    right = jnp.concatenate([x, p, ax, ap], axis=1)
    top = dot_split_tn(x, right)
    low = dot_split_tn(p, right[:, K:])
    parts = (
        top[:, 0:K],
        top[:, K : 2 * K],
        low[:, 0:K],
        top[:, 2 * K : 3 * K],
        top[:, 3 * K :],
        low[:, K : 2 * K],
        low[:, 2 * K :],
    )
    for i, part in enumerate(parts):
        out_ref[(2 + i) * K : (3 + i) * K, :] = part
    out_ref[9 * K :, :] = dot_split_tn(ap, ap)


def combine(first, second, third, d_ref):
    return dot_split(jnp.concatenate([first, second, third], axis=1), d_ref[...])


def side_kernel(x_ref, p_ref, ax_ref, d_ref, nx_ref, np_ref):
    final((x_ref, ax_ref, p_ref), d_ref, (np_ref, nx_ref))


def final(fields, d_ref, outs):
    new = combine(*(f[...] for f in fields), d_ref)
    np_ref, nx_ref = outs
    np_ref[...] = new[:, :K]
    nx_ref[...] = new[:, K:]


def update(fields, hot_ref, d_ref, outs):
    new = combine(*(f[...] for f in fields), d_ref)
    nap_ref, nax_ref, *sent = outs
    nap_ref[...] = new[:, :K]
    new_ax = new[:, K:]
    nax_ref[...] = new_ax
    field = new_ax.astype(BF16)
    for d, out in enumerate(sent):
        hot = hot_ref[d * HALO : (d + 1) * HALO, :]
        out[...] = jnp.dot(hot, field, preferred_element_type=F32).astype(BF16)


def operator_body(
    fields, halos, tiles_ref, side_ref, row_ref, col_ref, count_ref, core_ref, outs, scratch
):
    q_ref, keep_ref, give_ref = outs
    ext_ref, acc_ref, pay_ref = scratch
    left = [f[...] for f in fields]
    apply_operator(
        left[1].astype(BF16), halos, tiles_ref, row_ref, col_ref, count_ref, ext_ref, acc_ref
    )
    q = acc_ref[...]
    if q_ref is not None:
        q_ref[...] = q
        left.insert(3, q)
    wide = dot_split_tn(q, jnp.concatenate(left, axis=1))
    for i in range(len(left)):
        pay_ref[i * K : (i + 1) * K, :] = wide[:, i * K : (i + 1) * K]
    if side_ref is not None:
        pay_ref[5 * K :, :] = side_ref[...]
    half = pay_ref.shape[0] // 2
    core = core_ref[0]
    keep_ref[...] = pay_ref[pl.ds(pl.multiple_of(core * half, 8), half), :]
    give_ref[...] = pay_ref[pl.ds(pl.multiple_of((1 - core) * half, 8), half), :]


def first_image_kernel(
    x_ref, ax_ref, p_ref, ap_ref, h0, h1, h2, h3, tiles_ref, side_ref,
    row_ref, col_ref, count_ref, core_ref, *rest,
):
    operator_body(
        (x_ref, ax_ref, p_ref, ap_ref), (h0, h1, h2, h3), tiles_ref, side_ref,
        row_ref, col_ref, count_ref, core_ref, rest[:3], rest[3:],
    )


def image_kernel(
    x_ref, ax_ref, p_ref, ap_ref, h0, h1, h2, h3, tiles_ref,
    row_ref, col_ref, count_ref, core_ref, after_ref, *rest,
):
    operator_body(
        (x_ref, ax_ref, p_ref, ap_ref), (h0, h1, h2, h3), tiles_ref, None,
        row_ref, col_ref, count_ref, core_ref, rest[:3], rest[3:],
    )


def last_image_kernel(
    x_ref, ax_ref, p_ref, h0, h1, h2, h3, tiles_ref,
    row_ref, col_ref, count_ref, core_ref, after_ref, *rest,
):
    operator_body(
        (x_ref, ax_ref, p_ref), (h0, h1, h2, h3), tiles_ref, None,
        row_ref, col_ref, count_ref, core_ref, (None,) + rest[:2], rest[2:],
    )


KNOWN = ("xx", "xp", "pp", "k", "xap", "pax", "pap")
IMAGES = ("axax", "axap", "apap")
STAGE1 = ("theta", "a1", "u12", "s22")
STAGE2 = (
    "gxr", "gpr", "v13", "thk", "zr1", "kth", "paxth", "thxap", "a2", "v23", "a21", "ath", "bth",
)
STAGE3 = ("grr", "hrx", "hrp", "l31", "l32", "l33", "m11", "m12", "m22")
ALL_STAGES = (KNOWN, STAGE1, STAGE2, STAGE3, IMAGES)


def reader(names, refs):
    place = {name: (ref, i) for group, ref in zip(names, refs) for i, name in enumerate(group)}

    def get(name):
        ref, i = place[name]
        return ref[i]

    return get


def put(names, ref, values):
    for i, name in enumerate(names):
        ref[i] = values[name]


def join_halves(own_ref, other_ref, core_ref, pay_ref):
    half = own_ref.shape[0]
    core = core_ref[0]
    pay_ref[pl.ds(pl.multiple_of(core * half, 8), half), :] = own_ref[...]
    pay_ref[pl.ds(pl.multiple_of((1 - core) * half, 8), half), :] = other_ref[...]


def stage1(get, sa, sb, sc, sd):
    ident = eye()
    xx, pp = get("xx"), get("pp")
    ex_c, ex_r = inv_scales(xx, ident)
    ep_c, ep_r = inv_scales(pp, ident)
    sa[...] = xx * ex_c * ex_r + RIDGE * ident
    sb[...] = ident
    sc[...] = xx
    sd[...] = sym(get("k"))
    eliminate([(sa, sb, False), (sc, sd, True)], False)
    a1 = sb[...] * ex_r
    u12 = dot(a1, get("xp")) * ep_r
    s22 = pp * ep_c * ep_r + RIDGE * ident - dot_tn(u12, u12)
    return {"theta": sd[...], "a1": a1, "u12": u12, "s22": s22}


def stage2(get, sa, sb):
    ident = eye()
    sa[...] = get("s22")
    sb[...] = ident
    theta, a1, u12, k, pax = get("theta"), get("a1"), get("u12"), get("k"), get("pax")
    gxr = k - dot(get("xx"), theta)
    gpr = pax - dot_tn(get("xp"), theta)
    v13 = dot(a1, gxr)
    thk = dot_tn(theta, k)
    out = {
        "gxr": gxr,
        "gpr": gpr,
        "v13": v13,
        "thk": thk,
        "zr1": thk + dot_tn(gxr, theta),
        "kth": dot(k, theta),
        "paxth": dot(pax, theta),
        "thxap": dot_tn(theta, get("xap")),
        "ath": dot(get("axax"), theta),
        "bth": dot_tn(get("axap"), theta),
    }
    low = dot_tn(u12, jnp.concatenate([v13, a1], axis=1))
    ep_r = inv_scales(get("pp"), ident)[1]
    eliminate([(sa, sb, False)])
    y2 = sb[...]
    out["a2"] = y2 * ep_r
    out["v23"] = dot(y2, gpr * inv_scales(get("pp"), ident)[0] - low[:, :K])
    out["a21"] = -dot(y2, low[:, K:])
    return out


def stage3(get, sa, sb):
    ident = eye()
    a1, a2, a21, v13, v23 = (get(n) for n in ("a1", "a2", "a21", "v13", "v23"))
    one = dot_tn(v13, jnp.concatenate([v13, a1], axis=1))
    two = dot_tn(v23, jnp.concatenate([v23, a21, a2], axis=1))
    h12 = 0.5 * (get("xap") + get("pax").T)
    left = jnp.concatenate(
        [
            jnp.concatenate([a1, jnp.zeros_like(a1)], axis=1),
            jnp.concatenate([a21, a2], axis=1),
        ],
        axis=0,
    )
    mid = jnp.concatenate(
        [
            jnp.concatenate([sym(get("k")), h12], axis=1),
            jnp.concatenate([h12.T, sym(get("pap"))], axis=1),
        ],
        axis=0,
    )
    grr = sym(get("axax") - get("zr1"))
    er_c, er_r = inv_scales(grr, ident)
    sa[...] = (grr - one[:, :K] - two[:, :K]) * er_c * er_r + RIDGE * ident
    sb[...] = ident
    mpp = dot_nt(dot(left, mid), left)
    eliminate([(sa, sb, False)])
    l33 = sb[...] * er_r
    both = jnp.concatenate([one[:, K:] + two[:, K : 2 * K], two[:, 2 * K :]], axis=1)
    both = -dot(l33, both)
    return {
        "grr": grr,
        "hrx": get("axax") - get("thk"),
        "hrp": get("axap") - get("thxap"),
        "l31": both[:, :K],
        "l32": both[:, K:],
        "l33": l33,
        "m11": mpp[:K, :K],
        "m12": mpp[:K, K:],
        "m22": mpp[K:, K:],
    }


def first_prepare_kernel(
    own_ref, other_ref, core_ref, r0, r1, r2, r3, r4, new_ref, pay_ref, sa, sb, sc, sd
):
    join_halves(own_ref, other_ref, core_ref, pay_ref)
    new_ref[...] = pay_ref[0 : 5 * K, :]
    for i in range(len(KNOWN)):
        r0[i] = pay_ref[(7 + i) * K : (8 + i) * K, :] * SCALE
    for i, block in enumerate((5, 6, 14)):
        r4[i] = pay_ref[block * K : (block + 1) * K, :] * SCALE
    get = reader(ALL_STAGES, (r0, r1, r2, r3, r4))
    put(STAGE1, r1, stage1(get, sa, sb, sc, sd))
    put(STAGE2, r2, stage2(get, sa, sb))
    put(STAGE3, r3, stage3(get, sa, sb))


def new_basis(c):
    top = jnp.concatenate([c[:K], jnp.zeros((K, K), F32)], axis=1)
    return jnp.concatenate([top, jnp.concatenate([c[K:], c[K:]], axis=1)], axis=0)


def known_kernel(g_ref, h_ref, c_ref, r0):
    both = new_basis(c_ref[...])
    gg = dot_tn(both, dot(g_ref[...], both))
    hh = dot_tn(both, dot(h_ref[...], both))
    values = (
        gg[:K, :K],
        gg[:K, K:],
        gg[K:, K:],
        hh[:K, :K],
        hh[:K, K:],
        hh[K:, :K],
        hh[K:, K:],
    )
    put(KNOWN, r0, dict(zip(KNOWN, values)))


def stage1_kernel(r0, after_ref, r1, sa, sb, sc, sd):
    put(STAGE1, r1, stage1(reader(ALL_STAGES[:1], (r0,)), sa, sb, sc, sd))


def stage2_kernel(n_ref, c_ref, r0, r1, after_ref, r2, r4, sa, sb):
    both = new_basis(c_ref[...])
    nn = dot_tn(both, dot(n_ref[...], both))
    put(IMAGES, r4, {"axax": nn[:K, :K], "axap": nn[:K, K:], "apap": nn[K:, K:]})
    get = reader((KNOWN, STAGE1, IMAGES), (r0, r1, r4))
    put(STAGE2, r2, stage2(get, sa, sb))


def stage3_kernel(r0, r1, r2, r4, after_ref, r3, sa, sb):
    get = reader((KNOWN, STAGE1, STAGE2, IMAGES), (r0, r1, r2, r4))
    put(STAGE3, r3, stage3(get, sa, sb))


def fill(ref, rows):
    for i, line in enumerate(rows):
        for j, value in enumerate(line):
            ref[i * K : (i + 1) * K, j * K : (j + 1) * K] = value


def solve(pay_ref, get, c_ref, d_ref, gram_refs, le, hs, sa, sb):
    new = [pay_ref[i * K : (i + 1) * K, :] * SCALE for i in range(5 if gram_refs else 3)]
    qx, qax, qp = new[:3]
    ident = eye()
    theta = get("theta")
    hrx, hrp = get("hrx"), get("hrp")
    xq, axq = qx.T, qax.T
    hxr = xq - get("kth")
    hpr = qp.T - get("paxth")
    hrr = axq - dot_tn(theta, xq) - dot(hrx, theta)
    h13 = 0.5 * (hxr + hrx.T)
    h23 = 0.5 * (hpr + hrp.T)
    h12 = 0.5 * (get("xap") + get("pax").T)
    zero = jnp.zeros((K, K), F32)
    fill(
        hs,
        (
            (sym(get("k")), h12, h13),
            (h12.T, sym(get("pap")), h23),
            (h13.T, h23.T, sym(hrr)),
        ),
    )
    fill(
        le,
        (
            (get("a1"), zero, zero),
            (get("a21"), get("a2"), zero),
            (get("l31"), get("l32"), get("l33")),
        ),
    )
    last = dot(le[...], dot_nt(hs[...], le[2 * K :, :]))
    m13, m23, m33 = last[:K], last[K : 2 * K], last[2 * K :]
    m11, m12, m22 = get("m11"), get("m12"), get("m22")
    square = (
        m11 * m11 + m22 * m22 + m33 * m33 + 2.0 * (m12 * m12 + m13 * m13 + m23 * m23)
    )
    scale = 1.0 / (jnp.sqrt(jnp.sum(square, keepdims=True)) + 1e-06)
    m11, m12, m13, m22, m23, m33 = (x * scale for x in (m11, m12, m13, m22, m23, m33))
    fill(hs, ((m11, m12, m13), (m12.T, m22, m23), (m13.T, m23.T, m33)))
    m = hs[...]
    start = jnp.concatenate([ident, zero, zero], axis=0)
    basis = start - m[:, :K]
    basis = basis - dot_split(m, basis)
    basis = basis - dot_split(m, basis)
    sa[...] = dot_split_tn(basis, basis)
    sb[...] = ident
    raw = dot_split_tn(le[...], basis)
    raw = jnp.concatenate([raw, dot(theta, raw[2 * K :])], axis=0)
    if gram_refs:
        g_ref, h_ref, n_ref = gram_refs
        xp, gxr, gpr, axap = get("xp"), get("gxr"), get("gpr"), get("axap")
        fill(g_ref, ((get("xx"), xp, gxr), (xp.T, get("pp"), gpr), (gxr.T, gpr.T, get("grr"))))
        fill(
            h_ref,
            ((get("k"), get("xap"), hxr), (get("pax"), get("pap"), hpr), (hrx, hrp, hrr)),
        )
        axr = axq - get("ath")
        apr = new[4].T - get("bth")
        arr = new[3] - dot(qax, theta) - dot_tn(theta, axr)
        fill(n_ref, ((get("axax"), axap, axr), (axap.T, get("apap"), apr), (axr.T, apr.T, arr)))
    eliminate([(sa, sb, False)])
    c = dot_nt(raw, sb[...])
    cx, cp, cr, low = c[:K], c[K : 2 * K], c[2 * K : 3 * K], -c[3 * K :]
    if c_ref is not None:
        c_ref[...] = c[: 3 * K]
    fill(d_ref, ((low, low + cx), (cr, cr), (cp, cp)))


def first_solve_kernel(
    new_ref, r0, r1, r2, r3, r4, ax_ref, q_ref, ap_ref, hot_ref,
    c_ref, d_ref, g_ref, h_ref, n_ref, nap_ref, nax_ref, o0, o1, o2, o3, le, hs, sa, sb,
):
    get = reader(ALL_STAGES, (r0, r1, r2, r3, r4))
    solve(new_ref, get, c_ref, d_ref, (g_ref, h_ref, n_ref), le, hs, sa, sb)
    update((ax_ref, q_ref, ap_ref), hot_ref, d_ref, (nap_ref, nax_ref, o0, o1, o2, o3))


def solve_kernel(
    own_ref, other_ref, core_ref, r0, r1, r2, r3, r4, ax_ref, q_ref, ap_ref, hot_ref,
    c_ref, d_ref, g_ref, h_ref, n_ref, nap_ref, nax_ref, o0, o1, o2, o3, pay_ref, le, hs, sa, sb,
):
    join_halves(own_ref, other_ref, core_ref, pay_ref)
    get = reader(ALL_STAGES, (r0, r1, r2, r3, r4))
    solve(pay_ref, get, c_ref, d_ref, (g_ref, h_ref, n_ref), le, hs, sa, sb)
    update((ax_ref, q_ref, ap_ref), hot_ref, d_ref, (nap_ref, nax_ref, o0, o1, o2, o3))


def last_solve_kernel(
    own_ref, other_ref, core_ref, r0, r1, r2, r3, r4, x_ref, ax_ref, p_ref,
    np_ref, nx_ref, pay_ref, le, hs, sa, sb, d_ref,
):
    join_halves(own_ref, other_ref, core_ref, pay_ref)
    get = reader(ALL_STAGES, (r0, r1, r2, r3, r4))
    solve(pay_ref, get, None, d_ref, None, le, hs, sa, sb)
    final((x_ref, ax_ref, p_ref), d_ref, (np_ref, nx_ref))


VM = pl.BlockSpec(memory_space=pltpu.VMEM)
SM = pl.BlockSpec(memory_space=pltpu.SMEM)


def shape(*dims, dtype=F32):
    return jax.ShapeDtypeStruct(dims, dtype)


def call(kernel, ins, outs, scratch, name, us=3):
    arrays = [a for a, _ in ins]
    return pl.pallas_call(
        kernel,
        out_shape=tuple(outs),
        in_specs=[s for _, s in ins],
        out_specs=tuple(VM for _ in outs),
        scratch_shapes=scratch,
        compiler_params=pltpu.CompilerParams(vmem_limit_bytes=VMEM_LIMIT),
        cost_estimate=pl.CostEstimate(
            flops=us * 10**9, bytes_accessed=0, transcendentals=0
        ),
        name=name,
    )(*arrays)


def v(*arrays):
    return [(a, VM) for a in arrays]


def s(*arrays):
    return [(a, SM) for a in arrays]


def coords(i):
    region, dom = divmod(i, 8)
    return [region // 4, region % 4, dom // 2, dom % 2]


def index(z, y, x, core):
    return ((z * 4 + y) * 4 + x) * 2 + core


def flip(dim, kind):
    out = []
    for i in range(128):
        at = coords(i)
        if dim == 3 or kind == 0:
            at[dim] ^= 1
        else:
            at[dim] = {1: 2, 2: 1, 3: 0, 0: 3}[at[dim]]
        out.append((i, index(*at)))
    return out


def after(first, second):
    second = dict(second)
    return [(i, second[j]) for i, j in first]


def send(x, perm):
    return lax.ppermute(x, AXES, perm)


def all_sum(keep, give):
    y = keep + send(give, flip(3, 0))
    third = y.shape[0] // 24 * 8
    parts = [y[:third], y[third : 2 * third], y[2 * third :]]
    for kind in (0, 1):
        for r in range(3):
            parts = [p + send(p, flip((2 - r - i) % 3, kind)) for i, p in enumerate(parts)]
    y = jnp.concatenate(parts, axis=0)
    return y, send(y, flip(3, 0))


def all_sum_beside(keep, give, stages):
    y = keep + send(give, flip(3, 0))
    done = ()
    rounds = (((2, 0), (1, 0)), ((0, 0), (2, 1)), ((1, 1), (0, 1)))
    for (one, two), stage in zip(rounds, stages):
        fa, fb = flip(*one), flip(*two)
        ga, gb, gab = send(y, fa), send(y, fb), send(y, after(fa, fb))
        new = tuple(stage(y[:8], done))
        ga, gb, gab, *new = lax.optimization_barrier((ga, gb, gab) + new)
        done = done + tuple(new)
        y = (y + ga) + (gb + gab)
    return y, send(y, flip(3, 0)), done


def halo(outs):
    n_dom, n_region = 8, 16
    up = [(i, (i + 1) % n_dom) for i in range(n_dom)]
    down = [(j, i) for i, j in up]
    north = [(i, i + 1) for i in range(n_region - 1)]
    south = [(j, i) for i, j in north]
    return (
        lax.ppermute(outs[0], "dom", up),
        lax.ppermute(outs[1], "dom", down),
        lax.ppermute(outs[2], "region", north),
        lax.ppermute(outs[3], "region", south),
    )


def body(x, p, tiles, tile_row, tile_col, tile_count, send_rows):
    tiles = tiles[0]
    where = s(tile_row[0], tile_col[0], tile_count)
    core = jnp.reshape(lax.axis_index("dom") % 2, (1,)).astype(jnp.int32)
    idx = jnp.broadcast_to(send_rows.reshape(4 * HALO, 1), (4 * HALO, K))
    outs = [shape(HALO, K, dtype=BF16)] * 4
    field = shape(ROWS, K)
    square = pltpu.VMEM((K, K), F32)
    big = pltpu.VMEM((3 * K, 3 * K), F32)
    ext = [pltpu.VMEM((3 * ROWS, K), BF16), pltpu.VMEM((ROWS, K), F32)]

    sent = call(
        first_gather_kernel,
        v(x, p, idx),
        [shape(HALO, 2 * K, dtype=BF16)] * 4,
        [],
        "first_gather",
    )
    got = halo(sent)
    ax, ap, *sent = call(
        first_operator_kernel,
        v(x, p, *got, tiles, idx) + where,
        [field, field] + outs,
        [pltpu.VMEM((3 * ROWS, 2 * K), BF16), pltpu.VMEM((ROWS, 2 * K), F32)],
        "first_operator",
        5,
    )
    sizes = [shape(len(names), K, K) for names in ALL_STAGES]
    for it in range(ITERS):
        got = halo(sent)
        if it == 0:
            (hot,) = call(
                hot_kernel, v(idx), [shape(4 * HALO, ROWS, dtype=BF16)], [], "hot", 1
            )
            (side,) = call(
                first_side_kernel, v(x, p, ax, ap), [shape(10 * K, K)], [], "first_side", 2
            )
        else:
            x, p = call(side_kernel, v(x, p, old_ax, d), [field, field], [], "side", 1)
            (r0,) = call(known_kernel, v(g, h, c), sizes[:1], [], "known", 4)
        last = it + 1 == ITERS
        pay = (15, 5, 3)[it] * K
        res = call(
            (first_image_kernel, image_kernel, last_image_kernel)[it],
            v(x, ax, p)
            + ([] if last else v(ap))
            + v(*got, tiles)
            + (v(side) if it == 0 else [])
            + where
            + s(core)
            + ([] if it == 0 else [(r0, pl.BlockSpec(memory_space=pl.ANY))]),
            ([] if last else [field]) + [shape(pay // 2, K)] * 2,
            ext + [pltpu.VMEM((pay, K), F32)],
            "image",
        )
        *q, keep, give = res
        coef = [shape(3 * K, K), shape(3 * K, 2 * K)]
        gram = [shape(3 * K, 3 * K)] * 3
        scratch = [big, big, square, square]
        pay_scratch = [pltpu.VMEM((pay, K), F32)]
        if it == 0:
            own, other = all_sum(keep, give)
            *st, new = call(
                first_prepare_kernel,
                v(own, other) + s(core),
                sizes + [shape(5 * K, K)],
                pay_scratch + [square] * 4,
                "first_prepare",
            )
            c, d, g, h, n, *fields = call(
                first_solve_kernel,
                v(new, *st, ax, *q, ap, hot),
                coef + gram + [field, field] + outs,
                scratch,
                "first_solve",
            )
        else:

            def one(y, done):
                return call(stage1_kernel, v(r0, y), sizes[1:2], [square] * 4, "stage1", 7)

            def two(y, done):
                return call(
                    stage2_kernel,
                    v(n, c, r0, *done, y),
                    [sizes[2], sizes[4]],
                    [square] * 2,
                    "stage2",
                    6,
                )

            def three(y, done):
                return call(
                    stage3_kernel, v(r0, *done, y), sizes[3:4], [square] * 2, "stage3", 4
                )

            own, other, done = all_sum_beside(keep, give, (one, two, three))
            r1, r2, r4, r3 = done
            small = v(own, other) + s(core) + v(r0, r1, r2, r3, r4)
            if last:
                p, x = call(
                    last_solve_kernel,
                    small + v(x, ax, p),
                    [field, field],
                    pay_scratch + scratch + [pltpu.VMEM((3 * K, 2 * K), F32)],
                    "last_solve",
                )
                break
            c, d, g, h, n, *fields = call(
                solve_kernel,
                small + v(ax, *q, ap, hot),
                coef + gram + [field, field] + outs,
                pay_scratch + scratch,
                "solve",
            )
        old_ax = ax
        ap, ax, *sent = fields
    return x, p


def solution(mesh):
    in_specs = (
        P(AXES, None),
        P(AXES, None),
        P(AXES, None, None, None),
        P(AXES, None),
        P(AXES, None),
        P(AXES),
        P(AXES, None, None),
    )
    out_specs = (P(AXES, None), P(AXES, None))
    return jax.shard_map(body, mesh=mesh, in_specs=in_specs, out_specs=out_specs, check_vma=False)
```

```python
import jax
import jax.numpy as jnp
from jax import lax
from jax.experimental import pallas as pl
from jax.experimental.pallas import tpu as pltpu
from jax.sharding import PartitionSpec as P

K = 128
ITERS = 3
RIDGE = 0.001
NODES = 131072
ROWS = 1024
HALO = 512
CAP = 40
GROUP = 8
AXES = ("region", "dom")
F32 = jnp.float32
BF16 = jnp.bfloat16
SCALE = 1.0 / NODES
VMEM_LIMIT = 40 * 1024 * 1024


def dot(a, b):
    return jnp.dot(a, b, precision=lax.Precision.HIGHEST, preferred_element_type=F32)


def dot_tn(a, b):
    return lax.dot_general(
        a,
        b,
        (((0,), (0,)), ((), ())),
        precision=lax.Precision.HIGHEST,
        preferred_element_type=F32,
    )


def dot_nt(a, b):
    return lax.dot_general(
        a,
        b,
        (((1,), (1,)), ((), ())),
        precision=lax.Precision.HIGHEST,
        preferred_element_type=F32,
    )


def halves(m):
    high = m.astype(BF16)
    return high, (m - high.astype(F32)).astype(BF16)


def dot_split(a, b):
    a1, a2 = halves(a)
    b1, b2 = halves(b)
    return jnp.dot(
        jnp.concatenate([a1, a1, a2], axis=1),
        jnp.concatenate([b1, b2, b1], axis=0),
        preferred_element_type=F32,
    )


def dot_split_tn(a, b):
    a1, a2 = halves(a)
    b1, b2 = halves(b)
    return lax.dot_general(
        jnp.concatenate([a1, a1, a2], axis=0),
        jnp.concatenate([b1, b2, b1], axis=0),
        (((0,), (0,)), ((), ())),
        preferred_element_type=F32,
    )


def sym(m):
    return 0.5 * (m + m.T)


def eye():
    row = lax.broadcasted_iota(jnp.int32, (K, K), 0)
    col = lax.broadcasted_iota(jnp.int32, (K, K), 1)
    return jnp.where(row == col, 1.0, 0.0).astype(F32)


def inv_scales(m, ident):
    d = m * ident
    col = 1.0 / jnp.sqrt(jnp.sum(d, axis=1, keepdims=True) + 1e-06)
    row = 1.0 / jnp.sqrt(jnp.sum(d, axis=0, keepdims=True) + 1e-06)
    return col, row


def eliminate(systems, ahead=True):
    sub = lax.broadcasted_iota(jnp.int32, (8, K), 0)

    def row(x, t):
        return jnp.broadcast_to(x[t : t + 1, :], (8, K))

    def lane(x, j):
        return jnp.broadcast_to(x[:, j : j + 1], (8, K))

    def total(terms):
        while len(terms) > 1:
            terms = [terms[i] + terms[i + 1] for i in range(0, len(terms), 2)]
        return terms[0]

    def swap(x):
        return jnp.where(sub % 2 == 0, pltpu.roll(x, 7, 0), pltpu.roll(x, 1, 0))

    kept = [None] * len(systems)
    for p in range(K // 8):
        base = 8 * p
        for n, (a_ref, b_ref, full) in enumerate(systems):
            pa = a_ref[base : base + 8, :]
            pb = b_ref[base : base + 8, :]
            cols = kept[n]
            if cols is None:
                cols = [lane(pa, base + t) for t in range(8)]
            follow = [lane(pa, base + 8 + t) for t in range(8)] if ahead and p + 1 < K // 8 else []
            diag = jnp.zeros((8, K), F32)
            off = jnp.zeros((8, K), F32)
            low = pb
            for t in range(0, 8, 2):
                c0, c1 = cols[t], cols[t + 1]
                a, b, d = row(c0, t), row(c1, t), row(c1, t + 1)
                det = a * d - b * b
                rdet = 1.0 / det
                outside = (sub < t) | (sub > t + 1)
                m0 = jnp.where(outside, c0 * d - c1 * b, 0.0) * rdet
                m1 = jnp.where(outside, c1 * a - c0 * b, 0.0) * rdet
                for u in range(t + 2, 8):
                    cols[u] = cols[u] - (m0 * row(cols[u], t) + m1 * row(cols[u], t + 1))
                if not full:
                    ra = 1.0 / a
                    first, second = row(pb, t), row(pb, t + 1)
                    low = jnp.where(sub == t, first * lax.rsqrt(a), low)
                    low = jnp.where(
                        sub == t + 1, (second - first * (b * ra)) * lax.rsqrt(det * ra), low
                    )
                diag = jnp.where(sub == t, d * rdet, jnp.where(sub == t + 1, a * rdet, diag))
                off = jnp.where(outside, off, -b * rdet)
                pa = pa - (m0 * row(pa, t) + m1 * row(pa, t + 1))
                pb = pb - (m0 * row(pb, t) + m1 * row(pb, t + 1))
                follow = [f - (m0 * row(f, t) + m1 * row(f, t + 1)) for f in follow]
            pa = pa * diag + swap(pa) * off
            pb = pb * diag + swap(pb) * off
            follow = [f * diag + swap(f) * off for f in follow]
            ra = [row(pa, t) for t in range(8)]
            rb = [row(pb, t) for t in range(8)]
            kept[n] = None
            for i in range(K // 8):
                if i == p or (i < p and not full):
                    continue
                blk = a_ref[8 * i : 8 * i + 8, :]
                rhs = b_ref[8 * i : 8 * i + 8, :]
                c = [lane(blk, base + t) for t in range(8)]
                if follow and i == p + 1:
                    kept[n] = [
                        lane(blk, base + 8 + u) - total([c[t] * row(follow[u], t) for t in range(8)])
                        for u in range(8)
                    ]
                a_ref[8 * i : 8 * i + 8, :] = blk - total([c[t] * ra[t] for t in range(8)])
                b_ref[8 * i : 8 * i + 8, :] = rhs - total([c[t] * rb[t] for t in range(8)])
            if full:
                a_ref[base : base + 8, :] = pa
                b_ref[base : base + 8, :] = pb
            else:
                b_ref[base : base + 8, :] = low


def one_hot(picks, lanes):
    return jnp.concatenate(
        [jnp.where(picks == lanes + K * c, 1.0, 0.0).astype(BF16) for c in range(ROWS // K)],
        axis=1,
    )


def gather_rows(field, idx_ref, outs):
    lanes = lax.broadcasted_iota(jnp.int32, (HALO, K), 1)
    for d, out in enumerate(outs):
        hot = one_hot(idx_ref[d * HALO : (d + 1) * HALO, :], lanes)
        out[...] = jnp.dot(hot, field, preferred_element_type=F32).astype(BF16)


def hot_kernel(idx_ref, hot_ref):
    lanes = lax.broadcasted_iota(jnp.int32, (HALO, K), 1)
    for d in range(4):
        rows = slice(d * HALO, (d + 1) * HALO)
        hot_ref[rows, :] = one_hot(idx_ref[rows, :], lanes)


def apply_operator(own, halos, tiles_ref, row_ref, col_ref, count_ref, ext_ref, acc_ref):
    ext_ref[0:ROWS, :] = own
    for i, h in enumerate(halos):
        ext_ref[ROWS + i * HALO : ROWS + (i + 1) * HALO, :] = h[...]
    acc_ref[...] = jnp.zeros_like(acc_ref)
    count = count_ref[0]

    def group(g, carry):
        parts = []
        for j in range(GROUP):
            s = g * GROUP + j
            col = pl.multiple_of(col_ref[s] * K, K)
            prod = jnp.dot(tiles_ref[s], ext_ref[pl.ds(col, K), :], preferred_element_type=F32)
            parts.append(jnp.where(s < count, prod, 0.0))
        for j in range(GROUP):
            row = pl.multiple_of(row_ref[g * GROUP + j] * K, K)
            acc_ref[pl.ds(row, K), :] += parts[j]
        return carry

    lax.fori_loop(0, CAP // GROUP, group, 0)


def first_gather_kernel(x_ref, p_ref, idx_ref, *outs):
    both = jnp.concatenate([x_ref[...], p_ref[...]], axis=1).astype(BF16)
    gather_rows(both, idx_ref, outs)


def first_operator_kernel(
    x_ref, p_ref, h0, h1, h2, h3, tiles_ref, idx_ref, row_ref, col_ref, count_ref,
    ax_ref, ap_ref, o0, o1, o2, o3, ext_ref, acc_ref,
):
    own = jnp.concatenate([x_ref[...], p_ref[...]], axis=1).astype(BF16)
    apply_operator(
        own, (h0, h1, h2, h3), tiles_ref, row_ref, col_ref, count_ref, ext_ref, acc_ref
    )
    ax = acc_ref[:, :K]
    ax_ref[...] = ax
    ap_ref[...] = acc_ref[:, K:]
    gather_rows(ax.astype(BF16), idx_ref, (o0, o1, o2, o3))


def first_side_kernel(x_ref, p_ref, ax_ref, ap_ref, out_ref):
    x, p, ax, ap = x_ref[...], p_ref[...], ax_ref[...], ap_ref[...]
    wide = dot_split_tn(ax, jnp.concatenate([ax, ap], axis=1))
    out_ref[0:K, :] = wide[:, :K]
    out_ref[K : 2 * K, :] = wide[:, K:]
    right = jnp.concatenate([x, p, ax, ap], axis=1)
    top = dot_split_tn(x, right)
    low = dot_split_tn(p, right[:, K:])
    parts = (
        top[:, 0:K],
        top[:, K : 2 * K],
        low[:, 0:K],
        top[:, 2 * K : 3 * K],
        top[:, 3 * K :],
        low[:, K : 2 * K],
        low[:, 2 * K :],
    )
    for i, part in enumerate(parts):
        out_ref[(2 + i) * K : (3 + i) * K, :] = part
    out_ref[9 * K :, :] = dot_split_tn(ap, ap)


def combine(first, second, third, d_ref):
    return dot_split(jnp.concatenate([first, second, third], axis=1), d_ref[...])


def side_kernel(x_ref, p_ref, ax_ref, d_ref, nx_ref, np_ref):
    final((x_ref, ax_ref, p_ref), d_ref, (np_ref, nx_ref))


def final(fields, d_ref, outs):
    new = combine(*(f[...] for f in fields), d_ref)
    np_ref, nx_ref = outs
    np_ref[...] = new[:, :K]
    nx_ref[...] = new[:, K:]


def update(fields, hot_ref, d_ref, outs):
    new = combine(*(f[...] for f in fields), d_ref)
    nap_ref, nax_ref, *sent = outs
    nap_ref[...] = new[:, :K]
    new_ax = new[:, K:]
    nax_ref[...] = new_ax
    field = new_ax.astype(BF16)
    for d, out in enumerate(sent):
        hot = hot_ref[d * HALO : (d + 1) * HALO, :]
        out[...] = jnp.dot(hot, field, preferred_element_type=F32).astype(BF16)


def operator_body(
    fields, halos, tiles_ref, side_ref, row_ref, col_ref, count_ref, core_ref, outs, scratch
):
    q_ref, keep_ref, give_ref = outs
    ext_ref, acc_ref, pay_ref = scratch
    left = [f[...] for f in fields]
    apply_operator(
        left[1].astype(BF16), halos, tiles_ref, row_ref, col_ref, count_ref, ext_ref, acc_ref
    )
    q = acc_ref[...]
    if q_ref is not None:
        q_ref[...] = q
        left.insert(3, q)
    wide = dot_split_tn(q, jnp.concatenate(left, axis=1))
    for i in range(len(left)):
        pay_ref[i * K : (i + 1) * K, :] = wide[:, i * K : (i + 1) * K]
    if side_ref is not None:
        pay_ref[5 * K :, :] = side_ref[...]
    half = pay_ref.shape[0] // 2
    core = core_ref[0]
    keep_ref[...] = pay_ref[pl.ds(pl.multiple_of(core * half, 8), half), :]
    give_ref[...] = pay_ref[pl.ds(pl.multiple_of((1 - core) * half, 8), half), :]


def first_image_kernel(
    x_ref, ax_ref, p_ref, ap_ref, h0, h1, h2, h3, tiles_ref, side_ref,
    row_ref, col_ref, count_ref, core_ref, *rest,
):
    operator_body(
        (x_ref, ax_ref, p_ref, ap_ref), (h0, h1, h2, h3), tiles_ref, side_ref,
        row_ref, col_ref, count_ref, core_ref, rest[:3], rest[3:],
    )


def image_kernel(
    x_ref, ax_ref, p_ref, ap_ref, h0, h1, h2, h3, tiles_ref,
    row_ref, col_ref, count_ref, core_ref, after_ref, *rest,
):
    operator_body(
        (x_ref, ax_ref, p_ref, ap_ref), (h0, h1, h2, h3), tiles_ref, None,
        row_ref, col_ref, count_ref, core_ref, rest[:3], rest[3:],
    )


def last_image_kernel(
    x_ref, ax_ref, p_ref, h0, h1, h2, h3, tiles_ref,
    row_ref, col_ref, count_ref, core_ref, after_ref, *rest,
):
    operator_body(
        (x_ref, ax_ref, p_ref), (h0, h1, h2, h3), tiles_ref, None,
        row_ref, col_ref, count_ref, core_ref, (None,) + rest[:2], rest[2:],
    )


KNOWN = ("xx", "xp", "pp", "k", "xap", "pax", "pap")
IMAGES = ("axax", "axap", "apap")
STAGE1 = ("theta", "a1", "u12", "s22")
STAGE2 = (
    "gxr", "gpr", "v13", "thk", "zr1", "kth", "paxth", "thxap", "a2", "v23", "a21", "ath", "bth",
)
STAGE3 = ("grr", "hrx", "hrp", "l31", "l32", "l33", "m11", "m12", "m22")
ALL_STAGES = (KNOWN, STAGE1, STAGE2, STAGE3, IMAGES)


def reader(names, refs):
    place = {name: (ref, i) for group, ref in zip(names, refs) for i, name in enumerate(group)}

    def get(name):
        ref, i = place[name]
        return ref[i]

    return get


def put(names, ref, values):
    for i, name in enumerate(names):
        ref[i] = values[name]


def join_halves(own_ref, other_ref, core_ref, pay_ref):
    half = own_ref.shape[0]
    core = core_ref[0]
    pay_ref[pl.ds(pl.multiple_of(core * half, 8), half), :] = own_ref[...]
    pay_ref[pl.ds(pl.multiple_of((1 - core) * half, 8), half), :] = other_ref[...]


def stage1(get, sa, sb, sc, sd):
    ident = eye()
    xx, pp = get("xx"), get("pp")
    ex_c, ex_r = inv_scales(xx, ident)
    ep_c, ep_r = inv_scales(pp, ident)
    sa[...] = xx * ex_c * ex_r + RIDGE * ident
    sb[...] = ident
    sc[...] = xx
    sd[...] = sym(get("k"))
    eliminate([(sa, sb, False), (sc, sd, True)], False)
    a1 = sb[...] * ex_r
    u12 = dot(a1, get("xp")) * ep_r
    s22 = pp * ep_c * ep_r + RIDGE * ident - dot_tn(u12, u12)
    return {"theta": sd[...], "a1": a1, "u12": u12, "s22": s22}


def stage2(get, sa, sb):
    ident = eye()
    sa[...] = get("s22")
    sb[...] = ident
    theta, a1, u12, k, pax = get("theta"), get("a1"), get("u12"), get("k"), get("pax")
    gxr = k - dot(get("xx"), theta)
    gpr = pax - dot_tn(get("xp"), theta)
    v13 = dot(a1, gxr)
    thk = dot_tn(theta, k)
    out = {
        "gxr": gxr,
        "gpr": gpr,
        "v13": v13,
        "thk": thk,
        "zr1": thk + dot_tn(gxr, theta),
        "kth": dot(k, theta),
        "paxth": dot(pax, theta),
        "thxap": dot_tn(theta, get("xap")),
        "ath": dot(get("axax"), theta),
        "bth": dot_tn(get("axap"), theta),
    }
    low = dot_tn(u12, jnp.concatenate([v13, a1], axis=1))
    ep_r = inv_scales(get("pp"), ident)[1]
    eliminate([(sa, sb, False)])
    y2 = sb[...]
    out["a2"] = y2 * ep_r
    out["v23"] = dot(y2, gpr * inv_scales(get("pp"), ident)[0] - low[:, :K])
    out["a21"] = -dot(y2, low[:, K:])
    return out


def stage3(get, sa, sb):
    ident = eye()
    a1, a2, a21, v13, v23 = (get(n) for n in ("a1", "a2", "a21", "v13", "v23"))
    one = dot_tn(v13, jnp.concatenate([v13, a1], axis=1))
    two = dot_tn(v23, jnp.concatenate([v23, a21, a2], axis=1))
    h12 = 0.5 * (get("xap") + get("pax").T)
    left = jnp.concatenate(
        [
            jnp.concatenate([a1, jnp.zeros_like(a1)], axis=1),
            jnp.concatenate([a21, a2], axis=1),
        ],
        axis=0,
    )
    mid = jnp.concatenate(
        [
            jnp.concatenate([sym(get("k")), h12], axis=1),
            jnp.concatenate([h12.T, sym(get("pap"))], axis=1),
        ],
        axis=0,
    )
    grr = sym(get("axax") - get("zr1"))
    er_c, er_r = inv_scales(grr, ident)
    sa[...] = (grr - one[:, :K] - two[:, :K]) * er_c * er_r + RIDGE * ident
    sb[...] = ident
    mpp = dot_nt(dot(left, mid), left)
    eliminate([(sa, sb, False)])
    l33 = sb[...] * er_r
    both = jnp.concatenate([one[:, K:] + two[:, K : 2 * K], two[:, 2 * K :]], axis=1)
    both = -dot(l33, both)
    return {
        "grr": grr,
        "hrx": get("axax") - get("thk"),
        "hrp": get("axap") - get("thxap"),
        "l31": both[:, :K],
        "l32": both[:, K:],
        "l33": l33,
        "m11": mpp[:K, :K],
        "m12": mpp[:K, K:],
        "m22": mpp[K:, K:],
    }


def first_prepare_kernel(
    own_ref, other_ref, core_ref, r0, r1, r2, r3, r4, new_ref, pay_ref, sa, sb, sc, sd
):
    join_halves(own_ref, other_ref, core_ref, pay_ref)
    new_ref[...] = pay_ref[0 : 5 * K, :]
    for i in range(len(KNOWN)):
        r0[i] = pay_ref[(7 + i) * K : (8 + i) * K, :] * SCALE
    for i, block in enumerate((5, 6, 14)):
        r4[i] = pay_ref[block * K : (block + 1) * K, :] * SCALE
    get = reader(ALL_STAGES, (r0, r1, r2, r3, r4))
    put(STAGE1, r1, stage1(get, sa, sb, sc, sd))
    put(STAGE2, r2, stage2(get, sa, sb))
    put(STAGE3, r3, stage3(get, sa, sb))


def new_basis(c):
    top = jnp.concatenate([c[:K], jnp.zeros((K, K), F32)], axis=1)
    return jnp.concatenate([top, jnp.concatenate([c[K:], c[K:]], axis=1)], axis=0)


def known_kernel(g_ref, h_ref, c_ref, r0):
    both = new_basis(c_ref[...])
    gg = dot_tn(both, dot(g_ref[...], both))
    hh = dot_tn(both, dot(h_ref[...], both))
    values = (
        gg[:K, :K],
        gg[:K, K:],
        gg[K:, K:],
        hh[:K, :K],
        hh[:K, K:],
        hh[K:, :K],
        hh[K:, K:],
    )
    put(KNOWN, r0, dict(zip(KNOWN, values)))


def stage1_kernel(r0, after_ref, r1, sa, sb, sc, sd):
    put(STAGE1, r1, stage1(reader(ALL_STAGES[:1], (r0,)), sa, sb, sc, sd))


def stage2_kernel(n_ref, c_ref, r0, r1, after_ref, r2, r4, sa, sb):
    both = new_basis(c_ref[...])
    nn = dot_tn(both, dot(n_ref[...], both))
    put(IMAGES, r4, {"axax": nn[:K, :K], "axap": nn[:K, K:], "apap": nn[K:, K:]})
    get = reader((KNOWN, STAGE1, IMAGES), (r0, r1, r4))
    put(STAGE2, r2, stage2(get, sa, sb))


def stage3_kernel(r0, r1, r2, r4, after_ref, r3, sa, sb):
    get = reader((KNOWN, STAGE1, STAGE2, IMAGES), (r0, r1, r2, r4))
    put(STAGE3, r3, stage3(get, sa, sb))


def fill(ref, rows):
    for i, line in enumerate(rows):
        for j, value in enumerate(line):
            ref[i * K : (i + 1) * K, j * K : (j + 1) * K] = value


def solve(pay_ref, get, c_ref, d_ref, gram_refs, le, hs, sa, sb):
    new = [pay_ref[i * K : (i + 1) * K, :] * SCALE for i in range(5 if gram_refs else 3)]
    qx, qax, qp = new[:3]
    ident = eye()
    theta = get("theta")
    hrx, hrp = get("hrx"), get("hrp")
    xq, axq = qx.T, qax.T
    hxr = xq - get("kth")
    hpr = qp.T - get("paxth")
    hrr = axq - dot_tn(theta, xq) - dot(hrx, theta)
    h13 = 0.5 * (hxr + hrx.T)
    h23 = 0.5 * (hpr + hrp.T)
    h12 = 0.5 * (get("xap") + get("pax").T)
    zero = jnp.zeros((K, K), F32)
    fill(
        hs,
        (
            (sym(get("k")), h12, h13),
            (h12.T, sym(get("pap")), h23),
            (h13.T, h23.T, sym(hrr)),
        ),
    )
    fill(
        le,
        (
            (get("a1"), zero, zero),
            (get("a21"), get("a2"), zero),
            (get("l31"), get("l32"), get("l33")),
        ),
    )
    last = dot(le[...], dot_nt(hs[...], le[2 * K :, :]))
    m13, m23, m33 = last[:K], last[K : 2 * K], last[2 * K :]
    m11, m12, m22 = get("m11"), get("m12"), get("m22")
    square = (
        m11 * m11 + m22 * m22 + m33 * m33 + 2.0 * (m12 * m12 + m13 * m13 + m23 * m23)
    )
    scale = 1.0 / (jnp.sqrt(jnp.sum(square, keepdims=True)) + 1e-06)
    m11, m12, m13, m22, m23, m33 = (x * scale for x in (m11, m12, m13, m22, m23, m33))
    fill(hs, ((m11, m12, m13), (m12.T, m22, m23), (m13.T, m23.T, m33)))
    m = hs[...]
    start = jnp.concatenate([ident, zero, zero], axis=0)
    basis = start - m[:, :K]
    basis = basis - dot_split(m, basis)
    basis = basis - dot_split(m, basis)
    sa[...] = dot_split_tn(basis, basis)
    sb[...] = ident
    raw = dot_split_tn(le[...], basis)
    raw = jnp.concatenate([raw, dot(theta, raw[2 * K :])], axis=0)
    if gram_refs:
        g_ref, h_ref, n_ref = gram_refs
        xp, gxr, gpr, axap = get("xp"), get("gxr"), get("gpr"), get("axap")
        fill(g_ref, ((get("xx"), xp, gxr), (xp.T, get("pp"), gpr), (gxr.T, gpr.T, get("grr"))))
        fill(
            h_ref,
            ((get("k"), get("xap"), hxr), (get("pax"), get("pap"), hpr), (hrx, hrp, hrr)),
        )
        axr = axq - get("ath")
        apr = new[4].T - get("bth")
        arr = new[3] - dot(qax, theta) - dot_tn(theta, axr)
        fill(n_ref, ((get("axax"), axap, axr), (axap.T, get("apap"), apr), (axr.T, apr.T, arr)))
    eliminate([(sa, sb, False)])
    c = dot_nt(raw, sb[...])
    cx, cp, cr, low = c[:K], c[K : 2 * K], c[2 * K : 3 * K], -c[3 * K :]
    if c_ref is not None:
        c_ref[...] = c[: 3 * K]
    fill(d_ref, ((low, low + cx), (cr, cr), (cp, cp)))


def first_solve_kernel(
    new_ref, r0, r1, r2, r3, r4, ax_ref, q_ref, ap_ref, hot_ref,
    c_ref, d_ref, g_ref, h_ref, n_ref, nap_ref, nax_ref, o0, o1, o2, o3, le, hs, sa, sb,
):
    get = reader(ALL_STAGES, (r0, r1, r2, r3, r4))
    solve(new_ref, get, c_ref, d_ref, (g_ref, h_ref, n_ref), le, hs, sa, sb)
    update((ax_ref, q_ref, ap_ref), hot_ref, d_ref, (nap_ref, nax_ref, o0, o1, o2, o3))


def solve_kernel(
    own_ref, other_ref, core_ref, r0, r1, r2, r3, r4, ax_ref, q_ref, ap_ref, hot_ref,
    c_ref, d_ref, g_ref, h_ref, n_ref, nap_ref, nax_ref, o0, o1, o2, o3, pay_ref, le, hs, sa, sb,
):
    join_halves(own_ref, other_ref, core_ref, pay_ref)
    get = reader(ALL_STAGES, (r0, r1, r2, r3, r4))
    solve(pay_ref, get, c_ref, d_ref, (g_ref, h_ref, n_ref), le, hs, sa, sb)
    update((ax_ref, q_ref, ap_ref), hot_ref, d_ref, (nap_ref, nax_ref, o0, o1, o2, o3))


def last_solve_kernel(
    own_ref, other_ref, core_ref, r0, r1, r2, r3, r4, x_ref, ax_ref, p_ref,
    np_ref, nx_ref, pay_ref, le, hs, sa, sb, d_ref,
):
    join_halves(own_ref, other_ref, core_ref, pay_ref)
    get = reader(ALL_STAGES, (r0, r1, r2, r3, r4))
    solve(pay_ref, get, None, d_ref, None, le, hs, sa, sb)
    final((x_ref, ax_ref, p_ref), d_ref, (np_ref, nx_ref))


VM = pl.BlockSpec(memory_space=pltpu.VMEM)
SM = pl.BlockSpec(memory_space=pltpu.SMEM)


def shape(*dims, dtype=F32):
    return jax.ShapeDtypeStruct(dims, dtype)


def call(kernel, ins, outs, scratch, name, us=3):
    arrays = [a for a, _ in ins]
    return pl.pallas_call(
        kernel,
        out_shape=tuple(outs),
        in_specs=[s for _, s in ins],
        out_specs=tuple(VM for _ in outs),
        scratch_shapes=scratch,
        compiler_params=pltpu.CompilerParams(vmem_limit_bytes=VMEM_LIMIT),
        cost_estimate=pl.CostEstimate(
            flops=us * 10**9, bytes_accessed=0, transcendentals=0
        ),
        name=name,
    )(*arrays)


def v(*arrays):
    return [(a, VM) for a in arrays]


def s(*arrays):
    return [(a, SM) for a in arrays]


def coords(i):
    region, dom = divmod(i, 8)
    return [region // 4, region % 4, dom // 2, dom % 2]


def index(z, y, x, core):
    return ((z * 4 + y) * 4 + x) * 2 + core


def flip(dim, kind):
    out = []
    for i in range(128):
        at = coords(i)
        if dim == 3 or kind == 0:
            at[dim] ^= 1
        else:
            at[dim] = {1: 2, 2: 1, 3: 0, 0: 3}[at[dim]]
        out.append((i, index(*at)))
    return out


def after(first, second):
    second = dict(second)
    return [(i, second[j]) for i, j in first]


def send(x, perm):
    return lax.ppermute(x, AXES, perm)


def all_sum(keep, give):
    y = keep + send(give, flip(3, 0))
    third = y.shape[0] // 24 * 8
    parts = [y[:third], y[third : 2 * third], y[2 * third :]]
    for kind in (0, 1):
        for r in range(3):
            parts = [p + send(p, flip((2 - r - i) % 3, kind)) for i, p in enumerate(parts)]
    y = jnp.concatenate(parts, axis=0)
    return y, send(y, flip(3, 0))


def all_sum_beside(keep, give, stages):
    y = keep + send(give, flip(3, 0))
    done = ()
    rounds = (((2, 0), (1, 0)), ((0, 0), (2, 1)), ((1, 1), (0, 1)))
    for (one, two), stage in zip(rounds, stages):
        fa, fb = flip(*one), flip(*two)
        ga, gb, gab = send(y, fa), send(y, fb), send(y, after(fa, fb))
        new = tuple(stage(y[:8], done))
        ga, gb, gab, *new = lax.optimization_barrier((ga, gb, gab) + new)
        done = done + tuple(new)
        y = (y + ga) + (gb + gab)
    return y, send(y, flip(3, 0)), done


def halo(outs):
    n_dom, n_region = 8, 16
    up = [(i, (i + 1) % n_dom) for i in range(n_dom)]
    down = [(j, i) for i, j in up]
    north = [(i, i + 1) for i in range(n_region - 1)]
    south = [(j, i) for i, j in north]
    below = lax.ppermute(outs[2], "region", north)
    above = lax.ppermute(outs[3], "region", south)
    left = lax.ppermute(outs[0], "dom", up)
    right = lax.ppermute(outs[1], "dom", down)
    return left, right, below, above


def body(x, p, tiles, tile_row, tile_col, tile_count, send_rows):
    tiles = tiles[0]
    where = s(tile_row[0], tile_col[0], tile_count)
    core = jnp.reshape(lax.axis_index("dom") % 2, (1,)).astype(jnp.int32)
    idx = jnp.broadcast_to(send_rows.reshape(4 * HALO, 1), (4 * HALO, K))
    outs = [shape(HALO, K, dtype=BF16)] * 4
    field = shape(ROWS, K)
    square = pltpu.VMEM((K, K), F32)
    big = pltpu.VMEM((3 * K, 3 * K), F32)
    ext = [pltpu.VMEM((3 * ROWS, K), BF16), pltpu.VMEM((ROWS, K), F32)]

    sent = call(
        first_gather_kernel,
        v(x, p, idx),
        [shape(HALO, 2 * K, dtype=BF16)] * 4,
        [],
        "first_gather",
    )
    got = halo(sent)
    ax, ap, *sent = call(
        first_operator_kernel,
        v(x, p, *got, tiles, idx) + where,
        [field, field] + outs,
        [pltpu.VMEM((3 * ROWS, 2 * K), BF16), pltpu.VMEM((ROWS, 2 * K), F32)],
        "first_operator",
        5,
    )
    sizes = [shape(len(names), K, K) for names in ALL_STAGES]
    for it in range(ITERS):
        got = halo(sent)
        if it == 0:
            (hot,) = call(
                hot_kernel, v(idx), [shape(4 * HALO, ROWS, dtype=BF16)], [], "hot", 1
            )
            (side,) = call(
                first_side_kernel, v(x, p, ax, ap), [shape(10 * K, K)], [], "first_side", 2
            )
        else:
            x, p = call(side_kernel, v(x, p, old_ax, d), [field, field], [], "side", 1)
            (r0,) = call(known_kernel, v(g, h, c), sizes[:1], [], "known", 4)
        last = it + 1 == ITERS
        pay = (15, 5, 3)[it] * K
        res = call(
            (first_image_kernel, image_kernel, last_image_kernel)[it],
            v(x, ax, p)
            + ([] if last else v(ap))
            + v(*got, tiles)
            + (v(side) if it == 0 else [])
            + where
            + s(core)
            + ([] if it == 0 else [(r0, pl.BlockSpec(memory_space=pl.ANY))]),
            ([] if last else [field]) + [shape(pay // 2, K)] * 2,
            ext + [pltpu.VMEM((pay, K), F32)],
            "image",
        )
        *q, keep, give = res
        coef = [shape(3 * K, K), shape(3 * K, 2 * K)]
        gram = [shape(3 * K, 3 * K)] * 3
        scratch = [big, big, square, square]
        pay_scratch = [pltpu.VMEM((pay, K), F32)]
        if it == 0:
            own, other = all_sum(keep, give)
            *st, new = call(
                first_prepare_kernel,
                v(own, other) + s(core),
                sizes + [shape(5 * K, K)],
                pay_scratch + [square] * 4,
                "first_prepare",
            )
            c, d, g, h, n, *fields = call(
                first_solve_kernel,
                v(new, *st, ax, *q, ap, hot),
                coef + gram + [field, field] + outs,
                scratch,
                "first_solve",
            )
        else:

            def one(y, done):
                return call(stage1_kernel, v(r0, y), sizes[1:2], [square] * 4, "stage1", 7)

            def two(y, done):
                return call(
                    stage2_kernel,
                    v(n, c, r0, *done, y),
                    [sizes[2], sizes[4]],
                    [square] * 2,
                    "stage2",
                    6,
                )

            def three(y, done):
                return call(
                    stage3_kernel, v(r0, *done, y), sizes[3:4], [square] * 2, "stage3", 4
                )

            own, other, done = all_sum_beside(keep, give, (one, two, three))
            r1, r2, r4, r3 = done
            small = v(own, other) + s(core) + v(r0, r1, r2, r3, r4)
            if last:
                p, x = call(
                    last_solve_kernel,
                    small + v(x, ax, p),
                    [field, field],
                    pay_scratch + scratch + [pltpu.VMEM((3 * K, 2 * K), F32)],
                    "last_solve",
                )
                break
            c, d, g, h, n, *fields = call(
                solve_kernel,
                small + v(ax, *q, ap, hot),
                coef + gram + [field, field] + outs,
                pay_scratch + scratch,
                "solve",
            )
        old_ax = ax
        ap, ax, *sent = fields
    return x, p


def solution(mesh):
    in_specs = (
        P(AXES, None),
        P(AXES, None),
        P(AXES, None, None, None),
        P(AXES, None),
        P(AXES, None),
        P(AXES),
        P(AXES, None, None),
    )
    out_specs = (P(AXES, None), P(AXES, None))
    return jax.shard_map(body, mesh=mesh, in_specs=in_specs, out_specs=out_specs, check_vma=False)
```
